256 devices in a mesh: comp: 4 (over z_hi, core), lon: 16 (over x, y), lat: 4 (over z_lo).
Axes of the slice: x: 4, y: 4, z: 8 (z_hi: 2, z_lo: 4; z = z_hi * 4 + z_lo), core: 2. Of those that a mesh axis runs over, the one named last changes fastest.
Arguments:
- component_snapshots: bfloat16 [4, 16, 1440, 512], P('comp', 'lat', 'lon'), may hold values from -6 to 6
- cotangent: bfloat16 [4, 16, 1440, 512], P('comp', 'lat', 'lon'), may hold values from -0.15625 to 0.15625
- land: int32 [16, 1440], P('lat', 'lon'), may hold values 0 or 1
- atmosphere_kernel: float32 [49, 512], replicated, may hold values from -0.875 to 0.875
- atmosphere_gain: float32 [512], replicated, may hold values from 0.1 to 1.9
- atmosphere_expand_weight: bfloat16 [512, 2048], replicated, may hold values from -0.25 to 0.25
- atmosphere_contract_weight: bfloat16 [2048, 512], replicated, may hold values from -0.125 to 0.125
- ocean_kernel: float32 [49, 512], replicated, may hold values from -0.875 to 0.875
- ocean_gain: float32 [512], replicated, may hold values from 0.1 to 1.9
- ocean_expand_weight: bfloat16 [512, 2048], replicated, may hold values from -0.25 to 0.25
- ocean_contract_weight: bfloat16 [2048, 512], replicated, may hold values from -0.125 to 0.125
- marine_to_air_map: bfloat16 [512, 512], replicated, may hold values from -0.25 to 0.25
- flux_weight: bfloat16 [512, 512], replicated, may hold values from -0.25 to 0.25
Outputs:
- outputs: bfloat16 [4, 16, 1440, 512], P('comp', 'lat', 'lon')
- grad_kern_atm: float32 [49, 512], replicated
- grad_gain_atm: float32 [512], replicated
- grad_w_in_atm: float32 [512, 2048], P(('lon', 'lat'))
- grad_w_out_atm: float32 [2048, 512], P(('lon', 'lat'))
- grad_kern_ocn: float32 [49, 512], replicated
- grad_gain_ocn: float32 [512], replicated
- grad_w_in_ocn: float32 [512, 2048], P(('lon', 'lat'))
- grad_w_out_ocn: float32 [2048, 512], P(('lon', 'lat'))
- seasurface_weight_gradient: float32 [512, 512], P(('lon', 'lat'))
- flux_weight_gradient: float32 [512, 512], P(('lon', 'lat'))
The draws below stay inside these ranges and needn't reach their ends.
Inputs may be any that keep to these rules, and one draw needn't show every extreme that they name: 1 marks land, 0 sea.
All inputs are finite; a program needn't handle non-finite values. No bound on the sum of `land` on one device may be relied on, other than what follows from the above.
Results may differ from the reference program's by a relative error of at most 0.009.
Values may be sent and summed in bfloat16 or wider, within the bound.
No kernel may reach another device: no remote copies, remote signals or barrier semaphores. Data moves between devices by JAX's collectives and lax.ppermute only.
A program may use at most 128 MiB of HBM per device.

```python
import math
import jax
import jax.numpy as jnp
from jax import lax

CHANNEL_COUNT = 512
H = 2048
MERIDIONAL_SPAN = 16
ZONAL_EXTENT = 1440
N_COMP = 4


def with_ends(entries, own_key, least, top_value):
    index_at = [jax.random.randint(jax.random.fold_in(own_key, axis), (), 0, length) for axis, length in enumerate(entries.shape)]
    main_axis = entries.shape.index(max(entries.shape))
    beside = index_at[:main_axis] + [(index_at[main_axis] + 1) % entries.shape[main_axis]] + index_at[main_axis + 1:]
    return entries.at[tuple(index_at)].set(least).at[tuple(beside)].set(top_value)


def block_scale(rng, extent, cuts, low, high):
    loudness, own = 1.0, jax.random.fold_in(rng, 6)
    for axis_at, shards_of in cuts:
        steps = jnp.exp(jax.random.uniform(jax.random.fold_in(own, axis_at), (shards_of,), jnp.float32, low / len(cuts), high / len(cuts)))
        loudness = loudness * jnp.repeat(steps, extent[axis_at] // shards_of).reshape([-1 if axis == axis_at else 1 for axis in range(len(extent))])
    return loudness


def noise(key, dims, deviation, bound, cuts=(), held_as=jnp.bfloat16):
    factor_of = block_scale(key, dims, cuts, -0.22, 0.18) if cuts else 1.0
    array = jax.random.normal(key, dims, jnp.float32) * deviation * factor_of
    return jnp.minimum(jnp.maximum(array, -bound), bound).astype(held_as)


def setup_inputs(seed: int = 0) -> dict:
    keys = jax.random.split(jax.random.key(seed), 14)
    return {
        "component_snapshots": noise(keys[0], (N_COMP, MERIDIONAL_SPAN, ZONAL_EXTENT, CHANNEL_COUNT), 1.0, 6.0, ((0, 4), (1, 4), (2, 16))),
        "cotangent": noise(keys[1], (N_COMP, MERIDIONAL_SPAN, ZONAL_EXTENT, CHANNEL_COUNT), 0.01, 0.15625, ((0, 4), (1, 4), (2, 16))),
        "land": with_ends((jax.random.randint(keys[2], (MERIDIONAL_SPAN, ZONAL_EXTENT), 0, 5) < 2).astype(jnp.int32), jax.random.fold_in(keys[2], 1), 0, 1),
        "atmosphere_kernel": noise(keys[3], (49, CHANNEL_COUNT), 49 ** -0.5, 0.875, (), jnp.float32),
        "atmosphere_gain": jnp.clip(1.0 + 0.18 * jax.random.normal(keys[4], (CHANNEL_COUNT,), jnp.float32), 0.1, 1.9),
        "atmosphere_expand_weight": noise(keys[5], (CHANNEL_COUNT, H), CHANNEL_COUNT ** -0.5, 0.25),
        "atmosphere_contract_weight": noise(keys[6], (H, CHANNEL_COUNT), H ** -0.5, 0.125),
        "ocean_kernel": noise(keys[7], (49, CHANNEL_COUNT), 49 ** -0.5, 0.875, (), jnp.float32),
        "ocean_gain": jnp.clip(1.0 + 0.18 * jax.random.normal(keys[8], (CHANNEL_COUNT,), jnp.float32), 0.1, 1.9),
        "ocean_expand_weight": noise(keys[9], (CHANNEL_COUNT, H), CHANNEL_COUNT ** -0.5, 0.25),
        "ocean_contract_weight": noise(keys[10], (H, CHANNEL_COUNT), H ** -0.5, 0.125),
        "marine_to_air_map": noise(keys[11], (CHANNEL_COUNT, CHANNEL_COUNT), CHANNEL_COUNT ** -0.5, 0.25),
        "flux_weight": noise(keys[12], (CHANNEL_COUNT, CHANNEL_COUNT), CHANNEL_COUNT ** -0.5, 0.25),
    }


tanh_scale = math.sqrt(2.0 / math.pi)
cubic_term = 0.044715
eps_norm = 1e-06

def gelu_value(values):
    inner = tanh_scale * (values + cubic_term * values * values * values)
    return 0.5 * values * (1.0 + jnp.tanh(inner))

def gelu_slope(values):
    inner = tanh_scale * (values + cubic_term * values * values * values)
    tangent = jnp.tanh(inner)
    return 0.5 * (1.0 + tangent) + 0.5 * values * (1.0 - tangent * tangent) * tanh_scale * (1.0 + 3.0 * cubic_term * values * values)

def apply_taps(padded, kernel, height, breadth):
    total = jnp.zeros((height, breadth, padded.shape[2]), jnp.float32)
    for u in range(7):
        for v in range(7):
            total = total + kernel[u * 7 + v] * padded[u:u + height, v:v + breadth]
    return total

def tap_grads(grad_conv, padded, height, breadth):
    pieces = []
    for u in range(7):
        for v in range(7):
            pieces.append(lax.optimization_barrier(jnp.sum(grad_conv * padded[u:u + height, v:v + breadth], axis=(0, 1))))
    return jnp.stack(pieces)

def block_forward(field, padded, kernel, gain, w_in, w_out, mask):
    height, breadth, hidden_breadth_dim = field.shape
    conv = apply_taps(padded.astype(jnp.float32), kernel, height, breadth)
    centred = conv - lax.optimization_barrier(jnp.mean(conv, axis=2, keepdims=True))
    scale = lax.rsqrt(lax.optimization_barrier(jnp.mean(centred * centred, axis=2, keepdims=True)) + eps_norm)
    normed = centred * scale
    flat_norm = (normed * gain).astype(jnp.bfloat16).reshape(height * breadth, hidden_breadth_dim)
    pre_act = jnp.dot(flat_norm, w_in, preferred_element_type=jnp.float32)
    hidden = gelu_value(pre_act).astype(jnp.bfloat16)
    branch = jnp.dot(hidden, w_out, preferred_element_type=jnp.float32).reshape(height, breadth, hidden_breadth_dim)
    result = (field.astype(jnp.float32) + mask[:, :, None] * branch).astype(jnp.bfloat16)
    return (result, (normed, scale, flat_norm, pre_act, hidden))

def branch_backward(grad_out, gain, w_in, w_out, mask, saved):
    normed, scale, flat_norm, pre_act, hidden = saved
    height, breadth, hidden_breadth_dim = grad_out.shape
    grad_field = grad_out.astype(jnp.float32)
    grad_branch = (mask[:, :, None] * grad_field).astype(jnp.bfloat16).reshape(height * breadth, hidden_breadth_dim)
    grad_w_out = lax.dot_general(hidden, grad_branch, (((0,), (0,)), ((), ())), preferred_element_type=jnp.float32)
    grad_hidden = lax.dot_general(grad_branch, w_out, (((1,), (1,)), ((), ())), preferred_element_type=jnp.float32)
    grad_pre = (grad_hidden * gelu_slope(pre_act)).astype(jnp.bfloat16)
    grad_w_in = lax.dot_general(flat_norm, grad_pre, (((0,), (0,)), ((), ())), preferred_element_type=jnp.float32)
    grad_norm = lax.dot_general(grad_pre, w_in, (((1,), (1,)), ((), ())), preferred_element_type=jnp.float32)
    grad_norm = grad_norm.reshape(height, breadth, hidden_breadth_dim)
    grad_gain = lax.optimization_barrier(jnp.sum(grad_norm * normed, axis=(0, 1)))
    grad_z = grad_norm * gain
    grad_conv = scale * (grad_z - lax.optimization_barrier(jnp.mean(grad_z, axis=2, keepdims=True)) - normed * lax.optimization_barrier(jnp.mean(grad_z * normed, axis=2, keepdims=True)))
    return (grad_field, grad_conv, grad_w_in, grad_w_out, grad_gain)

def pad_grid(field):
    cycle = jnp.concatenate([field[:, -3:], field, field[:, :3]], axis=1)
    edge = jnp.zeros((3,) + cycle.shape[1:], cycle.dtype)
    return jnp.concatenate([edge, cycle, edge], axis=0)

def reference(component_snapshots, cotangent, land, atmosphere_kernel, atmosphere_gain, atmosphere_expand_weight, atmosphere_contract_weight, ocean_kernel, ocean_gain, ocean_expand_weight, ocean_contract_weight, marine_to_air_map, flux_weight):
    hidden_breadth_dim = component_snapshots.shape[3]
    predicted_copies = N_COMP - 1
    sea = (1 - land).astype(jnp.float32)
    oceanic_quantities = component_snapshots[predicted_copies].reshape(MERIDIONAL_SPAN * ZONAL_EXTENT, hidden_breadth_dim)
    upper_water_heat = jnp.dot(oceanic_quantities, marine_to_air_map, preferred_element_type=jnp.float32).astype(jnp.bfloat16)
    summed_passage_speed = jnp.zeros((MERIDIONAL_SPAN * ZONAL_EXTENT, hidden_breadth_dim), jnp.float32)
    for perturbed_sample in range(predicted_copies):
        summed_passage_speed = summed_passage_speed + jnp.dot(component_snapshots[perturbed_sample].reshape(MERIDIONAL_SPAN * ZONAL_EXTENT, hidden_breadth_dim), flux_weight, preferred_element_type=jnp.float32)
    driving_of_air = upper_water_heat.astype(jnp.float32).reshape(MERIDIONAL_SPAN, ZONAL_EXTENT, hidden_breadth_dim)
    applied_push_liquid = (summed_passage_speed / predicted_copies).reshape(MERIDIONAL_SPAN, ZONAL_EXTENT, hidden_breadth_dim)
    ones_mask = jnp.ones((MERIDIONAL_SPAN, ZONAL_EXTENT), jnp.float32)
    results = []
    applied_push_derivs = []
    atmosphere_gradients = None
    ocean_gradients = None
    for perturbed_sample in range(N_COMP):
        if perturbed_sample == predicted_copies:
            kernel, gain, w_in, w_out, mask, forcing_input = (ocean_kernel, ocean_gain, ocean_expand_weight, ocean_contract_weight, sea, applied_push_liquid)
        else:
            kernel, gain, w_in, w_out, mask, forcing_input = (atmosphere_kernel, atmosphere_gain, atmosphere_expand_weight, atmosphere_contract_weight, ones_mask, driving_of_air)
        field = (component_snapshots[perturbed_sample].astype(jnp.float32) + sea[:, :, None] * forcing_input).astype(jnp.bfloat16)
        padded = pad_grid(field)
        result, saved = block_forward(field, padded, kernel, gain, w_in, w_out, mask)
        results.append(result)
        grad_field, grad_conv, grad_w_in, grad_w_out, grad_gain = branch_backward(cotangent[perturbed_sample], gain, w_in, w_out, mask, saved)
        grad_kern = tap_grads(grad_conv, padded.astype(jnp.float32), MERIDIONAL_SPAN, ZONAL_EXTENT)
        padded_grad = pad_grid(grad_conv.astype(jnp.bfloat16))
        grad_input = grad_field + apply_taps(padded_grad.astype(jnp.float32), kernel[::-1], MERIDIONAL_SPAN, ZONAL_EXTENT)
        applied_push_derivs.append(sea[:, :, None] * grad_input)
        terms = (grad_kern, grad_gain, grad_w_in, grad_w_out)
        if perturbed_sample == predicted_copies:
            ocean_gradients = terms
        elif atmosphere_gradients is None:
            atmosphere_gradients = terms
        else:
            atmosphere_gradients = tuple((first + second for first, second in zip(atmosphere_gradients, terms)))
    seasurface_terms = applied_push_derivs[0]
    for perturbed_sample in range(1, predicted_copies):
        seasurface_terms = seasurface_terms + applied_push_derivs[perturbed_sample]
    seasurface_backward = seasurface_terms.astype(jnp.bfloat16).reshape(MERIDIONAL_SPAN * ZONAL_EXTENT, hidden_breadth_dim)
    seasurface_weight_gradient = lax.dot_general(oceanic_quantities, seasurface_backward, (((0,), (0,)), ((), ())), preferred_element_type=jnp.float32)
    surface_stream_reverse = (applied_push_derivs[predicted_copies] / predicted_copies).astype(jnp.bfloat16).reshape(MERIDIONAL_SPAN * ZONAL_EXTENT, hidden_breadth_dim)
    flux_weight_gradient = jnp.zeros((hidden_breadth_dim, hidden_breadth_dim), jnp.float32)
    for perturbed_sample in range(predicted_copies):
        flux_weight_gradient = flux_weight_gradient + lax.dot_general(component_snapshots[perturbed_sample].reshape(MERIDIONAL_SPAN * ZONAL_EXTENT, hidden_breadth_dim), surface_stream_reverse, (((0,), (0,)), ((), ())), preferred_element_type=jnp.float32)
    outputs = jnp.stack(results)
    return (outputs, atmosphere_gradients[0], atmosphere_gradients[1], atmosphere_gradients[2], atmosphere_gradients[3], ocean_gradients[0], ocean_gradients[1], ocean_gradients[2], ocean_gradients[3], seasurface_weight_gradient, flux_weight_gradient)
```

```python
import math

import jax
import jax.numpy as jnp
from jax import lax
from jax.sharding import Mesh
from jax.sharding import PartitionSpec as P

tanh_scale = math.sqrt(2.0 / math.pi)
cubic_term = 0.044715
eps_norm = 1e-06
bf16 = jnp.bfloat16
f32 = jnp.float32

COMP = ("zh", "core")
LON = ("x", "y")


def ring(count, step):
    return [(i, (i + step) % count) for i in range(count)]


def with_halo(cells, axis, count, dim, width, closed):
    ends = count if closed else count - 1
    head = lax.slice_in_dim(cells, 0, width, axis=dim)
    tail = lax.slice_in_dim(cells, cells.shape[dim] - width, cells.shape[dim], axis=dim)
    return jnp.concatenate(
        [
            lax.ppermute(tail, axis, [(i, (i + 1) % count) for i in range(ends)]),
            cells,
            lax.ppermute(head, axis, [((i + 1) % count, i) for i in range(ends)]),
        ],
        axis=dim,
    )


def extend(field):
    widened = with_halo(field, LON, 16, 1, 3, True)
    return with_halo(widened, "lat", 4, 0, 3, False)


def gelu_value(values):
    inner = tanh_scale * (values + cubic_term * values * values * values)
    return 0.5 * values * (1.0 + jnp.tanh(inner))


def gelu_slope(values):
    inner = tanh_scale * (values + cubic_term * values * values * values)
    tangent = jnp.tanh(inner)
    return 0.5 * (1.0 + tangent) + 0.5 * values * (1.0 - tangent * tangent) * tanh_scale * (
        1.0 + 3.0 * cubic_term * values * values
    )


def apply_taps(padded, kernel, height, breadth):
    total = jnp.zeros((height, breadth, padded.shape[2]), f32)
    for u in range(7):
        for v in range(7):
            total = total + kernel[u * 7 + v] * padded[u : u + height, v : v + breadth]
    return total


def tap_grads(grad_conv, padded, height, breadth):
    pieces = []
    for u in range(7):
        for v in range(7):
            pieces.append(jnp.sum(grad_conv * padded[u : u + height, v : v + breadth], axis=(0, 1)))
    return jnp.stack(pieces)


def dot_tn(a, b):
    return lax.dot_general(a, b, (((0,), (0,)), ((), ())), preferred_element_type=f32)


def dot_nt(a, b):
    return lax.dot_general(a, b, (((1,), (1,)), ((), ())), preferred_element_type=f32)


def scatter_sum(parts, axis):
    me = lax.axis_index(axis)
    total = lax.dynamic_index_in_dim(parts, me, 0, keepdims=False).astype(f32)
    for step in (1, 2, 3):
        out = lax.dynamic_index_in_dim(parts, (me + step) % 4, 0, keepdims=False)
        total = total + lax.ppermute(out, axis, ring(4, step)).astype(f32)
    return total


def all_sum(block, axis):
    one, two, three = (lax.ppermute(block, axis, ring(4, step)).astype(f32) for step in (1, 2, 3))
    return (block.astype(f32) + two) + (one + three)


def on_device(
    component_snapshots,
    cotangent,
    land,
    atmosphere_kernel,
    atmosphere_gain,
    atmosphere_expand_weight,
    atmosphere_contract_weight,
    ocean_kernel,
    ocean_gain,
    ocean_expand_weight,
    ocean_contract_weight,
    marine_to_air_map,
    flux_weight,
):
    zh, core = lax.axis_index("zh"), lax.axis_index("core")
    is_ocean = (zh == 1) & (core == 1)
    copies = 3.0
    sea = (1 - land).astype(f32)
    local = component_snapshots[0]
    height, breadth, channels = local.shape
    cells = height * breadth

    beside = lax.ppermute(local, "core", ring(2, 1))
    pair_sum = (local.astype(f32) + beside.astype(f32)).astype(bf16)
    payload = jnp.where(zh == 0, pair_sum, jnp.where(core == 0, beside, local))
    half = lax.dynamic_slice_in_dim(payload, core * (height // 2), height // 2, axis=0)
    got = lax.ppermute(half, "zh", ring(2, 1))
    got_beside = lax.ppermute(got, "core", ring(2, 1))
    full = jnp.where(
        core == 0,
        jnp.concatenate([got, got_beside], axis=0),
        jnp.concatenate([got_beside, got], axis=0),
    )
    ocean_sum = (full.astype(f32) + beside.astype(f32)).astype(bf16)
    partner = jnp.where(zh == 0, full, jnp.where(core == 0, beside, ocean_sum))
    partner = partner.reshape(cells, channels)

    coupling = jnp.where(is_ocean, flux_weight, marine_to_air_map)
    kernel = jnp.where(is_ocean, ocean_kernel, atmosphere_kernel)
    gain = jnp.where(is_ocean, ocean_gain, atmosphere_gain)
    w_in = jnp.where(is_ocean, ocean_expand_weight, atmosphere_expand_weight)
    w_out = jnp.where(is_ocean, ocean_contract_weight, atmosphere_contract_weight)
    mask = jnp.where(is_ocean, sea, jnp.ones_like(sea))

    projected = jnp.dot(partner, coupling, preferred_element_type=f32)
    forcing = jnp.where(is_ocean, projected / copies, projected.astype(bf16).astype(f32))
    forcing = forcing.reshape(height, breadth, channels)
    field = (local.astype(f32) + sea[:, :, None] * forcing).astype(bf16)
    padded = extend(field).astype(f32)

    conv = apply_taps(padded, kernel, height, breadth)
    centred = conv - jnp.mean(conv, axis=2, keepdims=True)
    scale = lax.rsqrt(jnp.mean(centred * centred, axis=2, keepdims=True) + eps_norm)
    normed = centred * scale
    norm_in = (normed * gain).astype(bf16).reshape(cells, channels)
    pre_act = jnp.dot(norm_in, w_in, preferred_element_type=f32)
    hidden = gelu_value(pre_act).astype(bf16)
    branch = jnp.dot(hidden, w_out, preferred_element_type=f32).reshape(height, breadth, channels)
    result = (field.astype(f32) + mask[:, :, None] * branch).astype(bf16)

    grad_field = cotangent[0].astype(f32)
    grad_branch = (mask[:, :, None] * grad_field).astype(bf16).reshape(cells, channels)
    grad_w_out = dot_tn(hidden, grad_branch).astype(bf16)
    grad_pre = (dot_nt(grad_branch, w_out) * gelu_slope(pre_act)).astype(bf16)
    grad_w_in = dot_tn(norm_in, grad_pre).astype(bf16)
    grad_norm = dot_nt(grad_pre, w_in).reshape(height, breadth, channels)
    grad_gain = jnp.sum(grad_norm * normed, axis=(0, 1))
    grad_z = grad_norm * gain
    grad_conv = scale * (
        grad_z
        - jnp.mean(grad_z, axis=2, keepdims=True)
        - normed * jnp.mean(grad_z * normed, axis=2, keepdims=True)
    )

    in_x = scatter_sum(grad_w_in.reshape(4, 128, 2048), "x").astype(bf16)
    out_parts = grad_w_out.reshape(4, 4, 128, 512).transpose(1, 0, 2, 3)
    out_y = scatter_sum(out_parts, "y").astype(bf16)
    in_xy = scatter_sum(in_x.reshape(4, 32, 2048), "y").astype(bf16)
    out_xy = scatter_sum(out_y, "x").astype(bf16)

    padded_grad = extend(grad_conv.astype(bf16)).astype(f32)
    grad_kern = tap_grads(grad_conv, padded, height, breadth)
    small = jnp.concatenate([grad_kern, grad_gain[None], jnp.zeros((6, channels), f32)])
    small = all_sum(small.astype(bf16), "x").astype(bf16)
    small = all_sum(small, "y").astype(bf16)

    grad_input = grad_field + apply_taps(padded_grad, kernel[::-1], height, breadth)
    forced = sea[:, :, None] * grad_input / jnp.where(is_ocean, copies, 1.0)
    forced = forced.astype(bf16).reshape(cells, channels)
    grad_couple = dot_tn(partner, forced).astype(bf16).reshape(16, 32, channels)
    couple = lax.all_to_all(grad_couple, LON, 0, 0, tiled=True)
    couple = jnp.sum(couple.astype(f32), axis=0).astype(bf16)

    pieces = jnp.concatenate(
        [
            in_xy.reshape(4, 32, 512),
            out_xy.reshape(4, 32, 512),
            couple.reshape(4, 8, 512),
            jnp.broadcast_to(small[None], (4, 56, 512)),
        ],
        axis=1,
    )
    column = lax.all_to_all(
        jnp.concatenate([pieces, pieces], axis=0), ("zh", "lat"), 0, 0, tiled=True
    ).astype(f32)
    near, far = jnp.sum(column[:4], axis=0), jnp.sum(column[4:], axis=0)
    sums = jnp.stack([near, far])
    sums_beside = lax.ppermute(sums, "core", ring(2, 1))
    first = jnp.where(core == 0, sums, sums_beside)
    second = jnp.where(core == 0, sums_beside, sums)
    air = (first[0] + first[1]) + second[0]
    sea_part = second[1]

    def split(total):
        return (
            total[72:121],
            total[121],
            total[:32].reshape(8, 2048),
            total[32:64],
        )

    return (
        (result[None],)
        + split(air)
        + split(sea_part)
        + (air[64:72], sea_part[64:72])
    )


def solution(mesh):
    fine = Mesh(mesh.devices.reshape(2, 2, 4, 4, 4), ("zh", "core", "x", "y", "lat"))
    state = P(COMP, "lat", LON, None)
    rows = P(("x", "y", "lat"), None)
    in_specs = (state, state, P("lat", LON)) + (P(),) * 10
    out_specs = (state, P(), P(), rows, rows, P(), P(), rows, rows, rows, rows)
    return jax.shard_map(
        on_device, mesh=fine, in_specs=in_specs, out_specs=out_specs, check_vma=False
    )
```

```python
import math

import jax
import jax.numpy as jnp
from jax import lax
from jax.experimental import pallas as pl
from jax.experimental.pallas import tpu as pltpu
from jax.sharding import Mesh
from jax.sharding import PartitionSpec as P

tanh_scale = math.sqrt(2.0 / math.pi)
cubic_term = 0.044715
eps_norm = 1e-06
bf16 = jnp.bfloat16
f32 = jnp.float32

COMP = ("zh", "core")
LON = ("x", "y")


def ring(count, step):
    return [(i, (i + step) % count) for i in range(count)]


def scatter_sum(parts, axis, dim):
    me = lax.axis_index(axis)
    total = lax.dynamic_index_in_dim(parts, me, dim, keepdims=False).astype(f32)
    for step in (1, 2, 3):
        out = lax.dynamic_index_in_dim(parts, lax.rem(me + step, 4), dim, keepdims=False)
        total = total + lax.ppermute(out, axis, ring(4, step)).astype(f32)
    return total


def all_sum(block, axis):
    one, two, three = (lax.ppermute(block, axis, ring(4, step)).astype(f32) for step in (1, 2, 3))
    return (block.astype(f32) + two) + (one + three)


def lat_halo(tile):
    north = lax.ppermute(tile[1:4], "lat", [(i, i + 1) for i in range(3)])
    south = lax.ppermute(tile[0:3], "lat", [(i + 1, i) for i in range(3)])
    return north, south


def picker(rows, cols, group, stride):
    row = lax.broadcasted_iota(jnp.int32, (rows, cols), 0)
    col = lax.broadcasted_iota(jnp.int32, (rows, cols), 1)
    pick = lax.rem(row, group) * stride + lax.div(row, group)
    return (pick == col).astype(f32).astype(bf16)


def mm(a, b, dims=((1,), (0,))):
    return lax.dot_general(a, b, (dims, ((), ())), preferred_element_type=f32)


def block_kernel(
    ocean_ref,
    north_ref,
    own_ref,
    south_ref,
    cot_ref,
    mask_ref,
    kern_ref,
    gain_ref,
    w_in_air,
    w_out_air,
    w_in_sea,
    w_out_sea,
    result_ref,
    gwi_ref,
    gwo_ref,
    small_ref,
    gct_ref,
    w_in,
    w_out,
    taps_in,
    conv,
    normed,
    norm_in,
    norm_in_t,
    gb,
    branch,
    gnorm,
    sems,
):
    @pl.when(ocean_ref[0] == 1)
    def _():
        pltpu.make_async_copy(w_in_sea, w_in, sems.at[0]).start()
        pltpu.make_async_copy(w_out_sea, w_out, sems.at[1]).start()

    @pl.when(ocean_ref[0] == 0)
    def _():
        pltpu.make_async_copy(w_in_air, w_in, sems.at[0]).start()
        pltpu.make_async_copy(w_out_air, w_out, sems.at[1]).start()

    spread = picker(144, 96, 8, 12)
    for r in range(10):
        src = north_ref[r] if r < 3 else own_ref[r - 3] if r < 7 else south_ref[r - 7]
        q = mm(spread, src)
        for lb in range(4):
            taps_in[lb, r] = q[:, lb * 128 : lb * 128 + 128].reshape(18, 8, 128)
    order = picker(96, 96, 8, 12)
    for i in range(4):
        gb[i * 96 : i * 96 + 96, :] = mm(order, cot_ref[i]).astype(bf16)

    def conv_step(n, carry):
        lb, i = lax.div(n, 4), lax.rem(n, 4)
        acc = [None] * 12
        for u in range(7):
            q = [taps_in[lb, i + u, t] for t in range(18)]
            for v in range(7):
                k = kern_ref[lb, pl.ds(u * 7 + v, 1), :]
                for t in range(12):
                    term = k * q[t + v]
                    acc[t] = term if acc[t] is None else acc[t] + term
        lanes = pl.ds(pl.multiple_of(lb * 128, 128), 128)
        for t in range(12):
            conv[pl.ds(pl.multiple_of(i * 96 + t * 8, 8), 8), lanes] = acc[t]
        return carry

    lax.fori_loop(0, 16, conv_step, 0)

    gain = gain_ref[...]
    scales = []
    for i in range(4):
        rows = slice(i * 96, i * 96 + 96)
        c = conv[rows, :]
        centred = c - jnp.mean(c, axis=1, keepdims=True)
        scale = lax.rsqrt(jnp.mean(centred * centred, axis=1, keepdims=True) + eps_norm)
        z = centred * scale
        scales.append(scale)
        normed[rows, :] = z
        norm_in[rows, :] = (z * gain).astype(bf16)
    norm_in_t[...] = norm_in[...].T
    branch[...] = jnp.zeros_like(branch)
    gnorm[...] = jnp.zeros_like(gnorm)
    pltpu.make_async_copy(w_in_air, w_in, sems.at[0]).wait()
    pltpu.make_async_copy(w_out_air, w_out, sems.at[1]).wait()

    def mlp_step(n, carry):
        cols = pl.ds(pl.multiple_of(n * 256, 256), 256)
        wi, wo = w_in[:, cols], w_out[cols, :]
        pre = mm(norm_in[...], wi)
        square = pre * pre
        tangent = jnp.tanh(tanh_scale * (pre + cubic_term * square * pre))
        half = 0.5 * (1.0 + tangent)
        hidden = (pre * half).astype(bf16)
        slope = half + 0.5 * pre * (1.0 - tangent * tangent) * (
            tanh_scale * (1.0 + 3.0 * cubic_term * square)
        )
        gpre = (mm(gb[...], wo, ((1,), (1,))) * slope).astype(bf16)
        branch[...] += mm(hidden, wo)
        gnorm[...] += mm(gpre, wi, ((1,), (1,)))
        gwi_ref[:, cols] = mm(norm_in_t[...], gpre).astype(bf16)
        gwo_ref[cols, :] = mm(hidden, gb[...], ((0,), (0,))).astype(bf16)
        return carry

    lax.fori_loop(0, 8, mlp_step, 0)

    back = picker(96, 96, 12, 8)
    ggain = jnp.zeros((1, 512), f32)
    for i in range(4):
        rows = slice(i * 96, i * 96 + 96)
        field = jnp.concatenate(
            [taps_in[lb, 3 + i, 3:15].reshape(96, 128) for lb in range(4)], axis=1
        )
        m = mask_ref[rows, :]
        res = (field + jnp.concatenate([m] * 4, axis=1) * branch[rows, :]).astype(bf16)
        result_ref[i] = mm(back, res).astype(bf16)[:90]
        g, z = gnorm[rows, :], normed[rows, :]
        ggain = ggain + jnp.sum(g * z, axis=0, keepdims=True)
        g = g * gain
        conv[rows, :] = scales[i] * (
            g - jnp.mean(g, axis=1, keepdims=True) - z * jnp.mean(g * z, axis=1, keepdims=True)
        )

    to_nat = picker(96, 96, 12, 8)
    to_16 = picker(96, 96, 16, 6)
    shuffle = mm(to_16, to_nat).astype(bf16)
    for i in range(4):
        rows = slice(i * 96, i * 96 + 96)
        moved = mm(shuffle, conv[rows, :].astype(bf16)).astype(bf16)
        norm_in[rows, :] = moved
    gct_ref[...] = norm_in[...].T

    def kern_step(n, carry):
        lb, u = lax.div(n, 7), lax.rem(n, 7)
        lanes = pl.ds(pl.multiple_of(lb * 128, 128), 128)
        acc = [jnp.zeros((8, 128), f32)] * 7
        for i in range(4):
            q = [taps_in[lb, i + u, t] for t in range(18)]
            for t in range(12):
                g = conv[i * 96 + t * 8 : i * 96 + t * 8 + 8, lanes]
                for v in range(7):
                    acc[v] = acc[v] + g * q[t + v]
        rows = [jnp.sum(a, axis=0, keepdims=True) for a in acc] + [jnp.zeros((1, 128), f32)]
        small_ref[pl.ds(pl.multiple_of(u * 8, 8), 8), lanes] = jnp.concatenate(rows, axis=0)
        return carry

    lax.fori_loop(0, 28, kern_step, 0)
    small_ref[56:64, :] = jnp.concatenate([ggain, jnp.zeros((7, 512), f32)], axis=0)


def block(ocean, north, own, south, cot, mask, kern, gain, wia, woa, wis, wos):
    vmem = pl.BlockSpec(memory_space=pltpu.VMEM)
    hbm = pl.BlockSpec(memory_space=pl.ANY)
    flops = 2 * 6 * 384 * 512 * 2048
    return pl.pallas_call(
        block_kernel,
        out_shape=(
            jax.ShapeDtypeStruct((4, 90, 512), bf16),
            jax.ShapeDtypeStruct((512, 2048), bf16),
            jax.ShapeDtypeStruct((2048, 512), bf16),
            jax.ShapeDtypeStruct((64, 512), f32),
            jax.ShapeDtypeStruct((512, 384), bf16),
        ),
        in_specs=[pl.BlockSpec(memory_space=pltpu.SMEM)] + [vmem] * 7 + [hbm] * 4,
        out_specs=(vmem,) * 5,
        scratch_shapes=[
            pltpu.VMEM((512, 2048), bf16),
            pltpu.VMEM((2048, 512), bf16),
            pltpu.VMEM((4, 10, 18, 8, 128), f32),
            pltpu.VMEM((384, 512), f32),
            pltpu.VMEM((384, 512), f32),
            pltpu.VMEM((384, 512), bf16),
            pltpu.VMEM((512, 384), bf16),
            pltpu.VMEM((384, 512), bf16),
            pltpu.VMEM((384, 512), f32),
            pltpu.VMEM((384, 512), f32),
            pltpu.SemaphoreType.DMA((2,)),
        ],
        compiler_params=pltpu.CompilerParams(vmem_limit_bytes=40 * 1024 * 1024),
        cost_estimate=pl.CostEstimate(
            flops=flops, bytes_accessed=12 * 1024 * 1024, transcendentals=384 * 2048
        ),
        name="block_kernel",
    )(ocean, north, own, south, cot, mask, kern, gain, wia, woa, wis, wos)


def couple_kernel(north_ref, own_ref, south_ref, gct_ref, cot_ref, kern_ref, scale_ref, out_ref, rows16, acc, cot_t):
    spread = picker(192, 96, 16, 6)
    for r in range(10):
        src = north_ref[r] if r < 3 else own_ref[r - 3] if r < 7 else south_ref[r - 7]
        rows16[r] = mm(spread, src).astype(bf16)
    order = picker(96, 96, 16, 6)
    moved = [mm(order, cot_ref[i]).astype(bf16) for i in range(4)]
    cot_t[...] = jnp.concatenate(moved, axis=0).T
    acc[...] = mm(cot_t[...], rows16[3:7, 48:144, :].reshape(384, 512))

    def step(u, carry):
        for v in range(7):
            part = rows16[pl.ds(u, 4), v * 16 : v * 16 + 96, :].reshape(384, 512)
            k = kern_ref[u, :, v : v + 1]
            acc[...] += k * mm(gct_ref[...], part)
        return carry

    lax.fori_loop(0, 7, step, 0)
    out_ref[...] = (acc[...] * scale_ref[0]).T.astype(bf16)


def couple(north, own, south, gct, cot, kern_t, scale):
    vmem = pl.BlockSpec(memory_space=pltpu.VMEM)
    return pl.pallas_call(
        couple_kernel,
        out_shape=jax.ShapeDtypeStruct((512, 512), bf16),
        in_specs=[vmem] * 6 + [pl.BlockSpec(memory_space=pltpu.SMEM)],
        out_specs=vmem,
        scratch_shapes=[
            pltpu.VMEM((10, 192, 512), bf16),
            pltpu.VMEM((512, 512), f32),
            pltpu.VMEM((512, 384), bf16),
        ],
        compiler_params=pltpu.CompilerParams(vmem_limit_bytes=40 * 1024 * 1024),
        cost_estimate=pl.CostEstimate(
            flops=2 * 50 * 384 * 512 * 512, bytes_accessed=4 * 1024 * 1024, transcendentals=0
        ),
        name="couple_kernel",
    )(north, own, south, gct, cot, kern_t, scale)


def on_device(
    component_snapshots,
    cotangent,
    land,
    atmosphere_kernel,
    atmosphere_gain,
    atmosphere_expand_weight,
    atmosphere_contract_weight,
    ocean_kernel,
    ocean_gain,
    ocean_expand_weight,
    ocean_contract_weight,
    marine_to_air_map,
    flux_weight,
):
    zh, core = lax.axis_index("zh"), lax.axis_index("core")
    is_ocean = (zh == 1) & (core == 1)
    copies = 3.0
    sea = (1 - land).astype(f32)
    local = component_snapshots[0]

    marked = jnp.concatenate(
        [local, jnp.broadcast_to(sea.astype(bf16)[:, :, None], (4, 90, 128))], axis=2
    )
    west = lax.ppermute(marked[:, 87:], LON, ring(16, 1))
    east = lax.ppermute(marked[:, :3], LON, ring(16, -1))
    local = jnp.concatenate([west[:, :, :512], local, east[:, :, :512]], axis=1)
    sea_wide = jnp.concatenate(
        [west[:, :, 512].astype(f32), sea, east[:, :, 512].astype(f32)], axis=1
    )

    beside = lax.ppermute(local, "core", ring(2, 1))
    pair_sum = (local.astype(f32) + beside.astype(f32)).astype(bf16)
    payload = jnp.where(zh == 0, pair_sum, jnp.where(core == 0, beside, local))
    half = lax.dynamic_slice_in_dim(payload, core * 2, 2, axis=0)
    got = lax.ppermute(half, "zh", ring(2, 1))
    got_beside = lax.ppermute(got, "core", ring(2, 1))
    full = jnp.where(
        core == 0,
        jnp.concatenate([got, got_beside], axis=0),
        jnp.concatenate([got_beside, got], axis=0),
    )
    ocean_sum = (full.astype(f32) + beside.astype(f32)).astype(bf16)
    partner = jnp.where(zh == 0, full, jnp.where(core == 0, beside, ocean_sum))

    coupling = jnp.where(is_ocean, flux_weight, marine_to_air_map)
    kernel = jnp.where(is_ocean, ocean_kernel, atmosphere_kernel)
    gain = jnp.where(is_ocean, ocean_gain, atmosphere_gain)
    mask = jnp.where(is_ocean, sea, jnp.ones_like(sea))
    grad_branch = (mask[:, :, None] * cotangent[0].astype(f32)).astype(bf16)
    grad_branch = jnp.pad(grad_branch, ((0, 0), (0, 6), (0, 0)))
    mask = jnp.pad(mask, ((0, 0), (0, 6))).reshape(4, 8, 12).transpose(0, 2, 1).reshape(384, 1)
    mask = jnp.broadcast_to(mask, (384, 128))
    kernel_lanes = kernel.reshape(49, 4, 128).transpose(1, 0, 2)
    kernel_rows = jnp.pad(
        kernel.reshape(7, 7, 512).transpose(0, 2, 1), ((0, 0), (0, 0), (0, 1))
    )

    projected = jnp.dot(partner.reshape(384, 512), coupling, preferred_element_type=f32)
    forcing = jnp.where(is_ocean, projected / copies, projected.astype(bf16).astype(f32))
    field = local.astype(f32) + sea_wide[:, :, None] * forcing.reshape(4, 96, 512)
    field = field.astype(bf16)
    north, south = lat_halo(field)
    masked = (sea_wide[:, :, None] * partner.astype(f32)).astype(bf16)
    masked, north = lax.optimization_barrier((masked, north))
    masked_north, masked_south = lat_halo(masked)

    result, grad_w_in, grad_w_out, small, grad_conv_t = block(
        is_ocean.astype(jnp.int32).reshape(1),
        north,
        field,
        south,
        grad_branch,
        mask,
        kernel_lanes,
        gain[None],
        atmosphere_expand_weight,
        atmosphere_contract_weight,
        ocean_expand_weight,
        ocean_contract_weight,
    )

    in_x = scatter_sum(grad_w_in.reshape(4, 128, 2048), "x", 0).astype(bf16)
    out_y = scatter_sum(grad_w_out.reshape(4, 4, 128, 512), "y", 1).astype(bf16)
    small = all_sum(small.astype(bf16), "x").astype(bf16)

    grad_couple = couple(
        masked_north,
        masked,
        masked_south,
        grad_conv_t,
        grad_branch,
        kernel_rows,
        jnp.where(is_ocean, 1.0 / copies, 1.0).astype(f32).reshape(1),
    )
    gathered = lax.all_to_all(grad_couple.reshape(16, 32, 512), LON, 0, 0, tiled=True)
    in_xy = scatter_sum(in_x.reshape(4, 32, 2048), "y", 0).astype(bf16)
    out_xy = scatter_sum(out_y, "x", 0).astype(bf16)
    small = all_sum(small, "y").astype(bf16)
    gathered = jnp.sum(gathered.astype(f32), axis=0).astype(bf16)

    pieces = jnp.concatenate(
        [
            in_xy.reshape(4, 32, 512),
            out_xy.reshape(4, 32, 512),
            gathered.reshape(4, 8, 512),
            jnp.broadcast_to(small[None], (4, 64, 512)),
        ],
        axis=1,
    )
    column = lax.all_to_all(
        jnp.concatenate([pieces, pieces], axis=0), ("zh", "lat"), 0, 0, tiled=True
    ).astype(f32)
    sums = jnp.stack([jnp.sum(column[:4], axis=0), jnp.sum(column[4:], axis=0)])
    sums_beside = lax.ppermute(sums, "core", ring(2, 1))
    first = jnp.where(core == 0, sums, sums_beside)
    second = jnp.where(core == 0, sums_beside, sums)
    air = (first[0] + first[1]) + second[0]
    sea_part = second[1]

    def split(total):
        return (
            total[72:128].reshape(7, 8, 512)[:, :7].reshape(49, 512),
            total[128],
            total[:32].reshape(8, 2048),
            total[32:64],
        )

    return (
        (result[None],)
        + split(air)
        + split(sea_part)
        + (air[64:72], sea_part[64:72])
    )


def solution(mesh):
    fine = Mesh(mesh.devices.reshape(2, 2, 4, 4, 4), ("zh", "core", "x", "y", "lat"))
    state = P(COMP, "lat", LON, None)
    rows = P(("x", "y", "lat"), None)
    in_specs = (state, state, P("lat", LON)) + (P(),) * 10
    out_specs = (state, P(), P(), rows, rows, P(), P(), rows, rows, rows, rows)
    return jax.shard_map(
        on_device, mesh=fine, in_specs=in_specs, out_specs=out_specs, check_vma=False
    )
```

```python
import math

import jax
import jax.numpy as jnp
from jax import lax
from jax.experimental import pallas as pl
from jax.experimental.pallas import tpu as pltpu
from jax.sharding import Mesh
from jax.sharding import PartitionSpec as P

tanh_scale = math.sqrt(2.0 / math.pi)
cubic_term = 0.044715
eps_norm = 1e-06
bf16 = jnp.bfloat16
f32 = jnp.float32

COMP = ("zh", "core")
LON = ("x", "y")


def ring(count, step):
    return [(i, (i + step) % count) for i in range(count)]


def cross(step, x_core):
    pairs = []
    for c in range(2):
        for x in range(4):
            for y in range(4):
                to = (x, (y + step) % 4) if c != x_core else ((x + step) % 4, y)
                pairs.append((c * 16 + x * 4 + y, c * 16 + to[0] * 4 + to[1]))
    return pairs


def total_of(parts):
    own, one, two, three = [part.astype(f32) for part in parts]
    return (own + two) + (one + three)


def place(parts, index):
    return lax.dynamic_index_in_dim(parts, index, 0, keepdims=False)


def lat_halo(tile):
    north = lax.ppermute(tile[1:4], "lat", [(i, i + 1) for i in range(3)])
    south = lax.ppermute(tile[0:3], "lat", [(i + 1, i) for i in range(3)])
    return north, south


def picker(rows, cols, group, stride):
    row = lax.broadcasted_iota(jnp.int32, (rows, cols), 0)
    col = lax.broadcasted_iota(jnp.int32, (rows, cols), 1)
    pick = lax.rem(row, group) * stride + lax.div(row, group)
    return (pick == col).astype(f32).astype(bf16)


def mm(a, b, dims=((1,), (0,))):
    return lax.dot_general(a, b, (dims, ((), ())), preferred_element_type=f32)


def block_kernel(
    ocean_ref,
    north_ref,
    own_ref,
    south_ref,
    cot_ref,
    mask_ref,
    kern_ref,
    gain_ref,
    w_in_air,
    w_out_air,
    w_in_sea,
    w_out_sea,
    result_ref,
    out_0,
    out_1,
    out_2,
    out_3,
    gct_ref,
    w_in,
    w_out,
    taps_in,
    conv,
    normed,
    norm_in,
    norm_in_t,
    gb,
    branch,
    gnorm,
    small,
    sems,
):
    outs = (out_0, out_1, out_2, out_3)
    here, far_step, near_step = ocean_ref[1], ocean_ref[2], ocean_ref[3]

    @pl.when(ocean_ref[0] == 1)
    def _():
        pltpu.make_async_copy(w_in_sea, w_in, sems.at[0]).start()
        pltpu.make_async_copy(w_out_sea, w_out, sems.at[1]).start()

    @pl.when(ocean_ref[0] == 0)
    def _():
        pltpu.make_async_copy(w_in_air, w_in, sems.at[0]).start()
        pltpu.make_async_copy(w_out_air, w_out, sems.at[1]).start()

    spread = picker(144, 96, 8, 12)
    for r in range(10):
        src = north_ref[r] if r < 3 else own_ref[r - 3] if r < 7 else south_ref[r - 7]
        q = mm(spread, src)
        for lb in range(4):
            taps_in[lb, r] = q[:, lb * 128 : lb * 128 + 128].reshape(18, 8, 128)
    order = picker(96, 96, 8, 12)
    for i in range(4):
        gb[i * 96 : i * 96 + 96, :] = mm(order, cot_ref[i]).astype(bf16)

    def conv_step(n, carry):
        lb, i = lax.div(n, 4), lax.rem(n, 4)
        acc = [None] * 12
        for u in range(7):
            q = [taps_in[lb, i + u, t] for t in range(18)]
            for v in range(7):
                k = kern_ref[lb, pl.ds(u * 7 + v, 1), :]
                for t in range(12):
                    term = k * q[t + v]
                    acc[t] = term if acc[t] is None else acc[t] + term
        lanes = pl.ds(pl.multiple_of(lb * 128, 128), 128)
        for t in range(12):
            conv[pl.ds(pl.multiple_of(i * 96 + t * 8, 8), 8), lanes] = acc[t]
        return carry

    lax.fori_loop(0, 16, conv_step, 0)

    gain = gain_ref[...]
    scales = []
    for i in range(4):
        rows = slice(i * 96, i * 96 + 96)
        c = conv[rows, :]
        centred = c - jnp.mean(c, axis=1, keepdims=True)
        scale = lax.rsqrt(jnp.mean(centred * centred, axis=1, keepdims=True) + eps_norm)
        z = centred * scale
        scales.append(scale)
        normed[rows, :] = z
        norm_in[rows, :] = (z * gain).astype(bf16)
    turned = norm_in[...].T
    for j in range(16):
        far = lax.rem(lax.div(j, far_step), 4)
        near = lax.rem(lax.div(j, near_step), 4)
        k = lax.rem(far + 4 - here, 4)
        rows = pl.ds(pl.multiple_of(k * 128 + near * 32, 32), 32)
        norm_in_t[rows, :] = turned[j * 32 : j * 32 + 32]
    branch[...] = jnp.zeros_like(branch)
    gnorm[...] = jnp.zeros_like(gnorm)
    pltpu.make_async_copy(w_in_air, w_in, sems.at[0]).wait()
    pltpu.make_async_copy(w_out_air, w_out, sems.at[1]).wait()

    def mlp_step(p, k):
        far = lax.rem(here + k, 4)
        blocks = [far * far_step + (2 * p + b) * near_step for b in (0, 1)]
        picked = [pl.ds(pl.multiple_of(block * 128, 128), 128) for block in blocks]
        wi = jnp.concatenate([w_in[:, cols] for cols in picked], axis=1)
        wo = jnp.concatenate([w_out[cols, :] for cols in picked], axis=0)
        pre = mm(norm_in[...], wi)
        square = pre * pre
        tangent = jnp.tanh(tanh_scale * (pre + cubic_term * square * pre))
        half = 0.5 * (1.0 + tangent)
        hidden = (pre * half).astype(bf16)
        slope = half + 0.5 * pre * (1.0 - tangent * tangent) * (
            tanh_scale * (1.0 + 3.0 * cubic_term * square)
        )
        gpre = (mm(gb[...], wo, ((1,), (1,))) * slope).astype(bf16)
        branch[...] += mm(hidden, wo)
        gnorm[...] += mm(gpre, wi, ((1,), (1,)))
        gwi = mm(norm_in_t[...], gpre).astype(bf16)
        gwo = mm(hidden, gb[...], ((0,), (0,))).astype(bf16)
        for b in (0, 1):
            lanes = pl.ds(pl.multiple_of(lax.rem(blocks[b], 4) * 128, 128), 128)
            band = lax.div(blocks[b], 4) * 32
            for j in range(4):
                for near in range(4):
                    rows = pl.ds(pl.multiple_of(near * 256 + band, 32), 32)
                    outs[j][rows, lanes] = gwi[
                        j * 128 + near * 32 : j * 128 + near * 32 + 32, b * 128 : b * 128 + 128
                    ]
            rows = pl.ds(pl.multiple_of((2 * p + b) * 256 + 128, 128), 128)
            outs[k][rows, :] = gwo[b * 128 : b * 128 + 128]

    for k in range(4):

        def pair_step(p, carry, k=k):
            mlp_step(p, k)
            return carry

        lax.fori_loop(0, 2, pair_step, 0)

    back = picker(96, 96, 12, 8)
    ggain = jnp.zeros((1, 512), f32)
    for i in range(4):
        rows = slice(i * 96, i * 96 + 96)
        field = jnp.concatenate(
            [taps_in[lb, 3 + i, 3:15].reshape(96, 128) for lb in range(4)], axis=1
        )
        m = mask_ref[rows, :]
        res = (field + jnp.concatenate([m] * 4, axis=1) * branch[rows, :]).astype(bf16)
        result_ref[i] = mm(back, res).astype(bf16)[:90]
        g, z = gnorm[rows, :], normed[rows, :]
        ggain = ggain + jnp.sum(g * z, axis=0, keepdims=True)
        g = g * gain
        conv[rows, :] = scales[i] * (
            g - jnp.mean(g, axis=1, keepdims=True) - z * jnp.mean(g * z, axis=1, keepdims=True)
        )

    to_nat = picker(96, 96, 12, 8)
    to_16 = picker(96, 96, 16, 6)
    shuffle = mm(to_16, to_nat).astype(bf16)
    for i in range(4):
        rows = slice(i * 96, i * 96 + 96)
        moved = mm(shuffle, conv[rows, :].astype(bf16)).astype(bf16)
        norm_in[rows, :] = moved
    gct_ref[...] = norm_in[...].T

    def kern_step(n, carry):
        lb, u = lax.div(n, 7), lax.rem(n, 7)
        lanes = pl.ds(pl.multiple_of(lb * 128, 128), 128)
        acc = [jnp.zeros((8, 128), f32)] * 7
        for i in range(4):
            q = [taps_in[lb, i + u, t] for t in range(18)]
            for t in range(12):
                g = conv[i * 96 + t * 8 : i * 96 + t * 8 + 8, lanes]
                for v in range(7):
                    acc[v] = acc[v] + g * q[t + v]
        rows = [jnp.sum(a, axis=0, keepdims=True) for a in acc] + [jnp.zeros((1, 128), f32)]
        small[pl.ds(pl.multiple_of(u * 8, 8), 8), lanes] = jnp.concatenate(rows, axis=0)
        return carry

    lax.fori_loop(0, 28, kern_step, 0)
    small[56:64, :] = jnp.concatenate([ggain, jnp.zeros((7, 512), f32)], axis=0)
    for out in outs:
        out[1024:1088, :] = small[...].astype(bf16)


def block(ocean, north, own, south, cot, mask, kern, gain, wia, woa, wis, wos):
    vmem = pl.BlockSpec(memory_space=pltpu.VMEM)
    hbm = pl.BlockSpec(memory_space=pl.ANY)
    flops = 2 * 6 * 384 * 512 * 2048
    return pl.pallas_call(
        block_kernel,
        out_shape=(
            jax.ShapeDtypeStruct((4, 90, 512), bf16),
            *[jax.ShapeDtypeStruct((1088, 512), bf16)] * 4,
            jax.ShapeDtypeStruct((512, 384), bf16),
        ),
        in_specs=[pl.BlockSpec(memory_space=pltpu.SMEM)] + [vmem] * 7 + [hbm] * 4,
        out_specs=(vmem,) * 6,
        scratch_shapes=[
            pltpu.VMEM((512, 2048), bf16),
            pltpu.VMEM((2048, 512), bf16),
            pltpu.VMEM((4, 10, 18, 8, 128), f32),
            pltpu.VMEM((384, 512), f32),
            pltpu.VMEM((384, 512), f32),
            pltpu.VMEM((384, 512), bf16),
            pltpu.VMEM((512, 384), bf16),
            pltpu.VMEM((384, 512), bf16),
            pltpu.VMEM((384, 512), f32),
            pltpu.VMEM((384, 512), f32),
            pltpu.VMEM((64, 512), f32),
            pltpu.SemaphoreType.DMA((2,)),
        ],
        compiler_params=pltpu.CompilerParams(vmem_limit_bytes=56 * 1024 * 1024),
        cost_estimate=pl.CostEstimate(
            flops=flops, bytes_accessed=12 * 1024 * 1024, transcendentals=384 * 2048
        ),
        name="block_kernel",
    )(ocean, north, own, south, cot, mask, kern, gain, wia, woa, wis, wos)


def couple_kernel(north_ref, own_ref, south_ref, gct_ref, cot_ref, kern_ref, scale_ref, out_ref, rows16, acc, cot_t):
    spread = picker(192, 96, 16, 6)
    for r in range(10):
        src = north_ref[r] if r < 3 else own_ref[r - 3] if r < 7 else south_ref[r - 7]
        rows16[r] = mm(spread, src).astype(bf16)
    order = picker(96, 96, 16, 6)
    moved = [mm(order, cot_ref[i]).astype(bf16) for i in range(4)]
    cot_t[...] = jnp.concatenate(moved, axis=0).T
    acc[...] = mm(cot_t[...], rows16[3:7, 48:144, :].reshape(384, 512))

    def step(u, carry):
        for v in range(7):
            part = rows16[pl.ds(u, 4), v * 16 : v * 16 + 96, :].reshape(384, 512)
            k = kern_ref[u, :, v : v + 1]
            acc[...] += k * mm(gct_ref[...], part)
        return carry

    lax.fori_loop(0, 7, step, 0)
    out_ref[...] = (acc[...] * scale_ref[0]).T.astype(bf16)


def couple(north, own, south, gct, cot, kern_t, scale):
    vmem = pl.BlockSpec(memory_space=pltpu.VMEM)
    return pl.pallas_call(
        couple_kernel,
        out_shape=jax.ShapeDtypeStruct((512, 512), bf16),
        in_specs=[vmem] * 6 + [pl.BlockSpec(memory_space=pltpu.SMEM)],
        out_specs=vmem,
        scratch_shapes=[
            pltpu.VMEM((10, 192, 512), bf16),
            pltpu.VMEM((512, 512), f32),
            pltpu.VMEM((512, 384), bf16),
        ],
        compiler_params=pltpu.CompilerParams(vmem_limit_bytes=56 * 1024 * 1024),
        cost_estimate=pl.CostEstimate(
            flops=2 * 50 * 384 * 512 * 512, bytes_accessed=4 * 1024 * 1024, transcendentals=0
        ),
        name="couple_kernel",
    )(north, own, south, gct, cot, kern_t, scale)


def on_device(
    component_snapshots,
    cotangent,
    land,
    atmosphere_kernel,
    atmosphere_gain,
    atmosphere_expand_weight,
    atmosphere_contract_weight,
    ocean_kernel,
    ocean_gain,
    ocean_expand_weight,
    ocean_contract_weight,
    marine_to_air_map,
    flux_weight,
):
    zh, core = lax.axis_index("zh"), lax.axis_index("core")
    is_ocean = (zh == 1) & (core == 1)
    copies = 3.0
    sea = (1 - land).astype(f32)
    local = component_snapshots[0]

    marked = jnp.concatenate(
        [local, jnp.broadcast_to(sea.astype(bf16)[:, :, None], (4, 90, 128))], axis=2
    )
    west = lax.ppermute(marked[:, 87:], LON, ring(16, 1))
    east = lax.ppermute(marked[:, :3], LON, ring(16, -1))
    local = jnp.concatenate([west[:, :, :512], local, east[:, :, :512]], axis=1)
    sea_wide = jnp.concatenate(
        [west[:, :, 512].astype(f32), sea, east[:, :, 512].astype(f32)], axis=1
    )

    beside = lax.ppermute(local, "core", ring(2, 1))
    pair_sum = (local.astype(f32) + beside.astype(f32)).astype(bf16)
    payload = jnp.where(zh == 0, pair_sum, jnp.where(core == 0, beside, local))
    half = lax.dynamic_slice_in_dim(payload, core * 2, 2, axis=0)
    got = lax.ppermute(half, "zh", ring(2, 1))
    got_beside = lax.ppermute(got, "core", ring(2, 1))
    full = jnp.where(
        core == 0,
        jnp.concatenate([got, got_beside], axis=0),
        jnp.concatenate([got_beside, got], axis=0),
    )
    ocean_sum = (full.astype(f32) + beside.astype(f32)).astype(bf16)
    partner = jnp.where(zh == 0, full, jnp.where(core == 0, beside, ocean_sum))

    coupling = jnp.where(is_ocean, flux_weight, marine_to_air_map)
    kernel = jnp.where(is_ocean, ocean_kernel, atmosphere_kernel)
    gain = jnp.where(is_ocean, ocean_gain, atmosphere_gain)
    mask = jnp.where(is_ocean, sea, jnp.ones_like(sea))
    grad_branch = (mask[:, :, None] * cotangent[0].astype(f32)).astype(bf16)
    grad_branch = jnp.pad(grad_branch, ((0, 0), (0, 6), (0, 0)))
    mask = jnp.pad(mask, ((0, 0), (0, 6))).reshape(4, 8, 12).transpose(0, 2, 1).reshape(384, 1)
    mask = jnp.broadcast_to(mask, (384, 128))
    kernel_lanes = kernel.reshape(49, 4, 128).transpose(1, 0, 2)
    kernel_rows = jnp.pad(
        kernel.reshape(7, 7, 512).transpose(0, 2, 1), ((0, 0), (0, 0), (0, 1))
    )

    projected = jnp.dot(partner.reshape(384, 512), coupling, preferred_element_type=f32)
    forcing = jnp.where(is_ocean, projected / copies, projected.astype(bf16).astype(f32))
    field = local.astype(f32) + sea_wide[:, :, None] * forcing.reshape(4, 96, 512)
    field = field.astype(bf16)
    north, south = lat_halo(field)
    masked = (sea_wide[:, :, None] * partner.astype(f32)).astype(bf16)
    masked, north = lax.optimization_barrier((masked, north))
    masked_north, masked_south = lat_halo(masked)

    x, y, lat = (lax.axis_index(axis) for axis in ("x", "y", "lat"))
    result, *parts, grad_conv_t = block(
        jnp.stack(
            [
                is_ocean.astype(jnp.int32),
                jnp.where(core == 0, x, y),
                jnp.where(core == 0, 4, 1),
                jnp.where(core == 0, 1, 4),
            ]
        ),
        north,
        field,
        south,
        grad_branch,
        mask,
        kernel_lanes,
        gain[None],
        atmosphere_expand_weight,
        atmosphere_contract_weight,
        ocean_expand_weight,
        ocean_contract_weight,
    )

    for k in (1, 2, 3):
        parts[k] = lax.ppermute(parts[k], ("core", "x", "y"), cross(k, 0))

    grad_couple = couple(
        masked_north,
        masked,
        masked_south,
        grad_conv_t,
        grad_branch,
        kernel_rows,
        jnp.where(is_ocean, 1.0 / copies, 1.0).astype(f32).reshape(1),
    )
    tables = [part[:1024].reshape(4, 256, 512) for part in parts]
    small = total_of([part[1024:] for part in parts])
    messages = []
    for k in range(4):
        table = total_of([place(t, lax.rem(jnp.where(core == 0, y, x) + k, 4)) for t in tables])
        messages.append(jnp.concatenate([table, small], axis=0).astype(bf16))
    for k in (1, 2, 3):
        messages[k] = lax.ppermute(messages[k], ("core", "x", "y"), cross(k, 1))
    gathered = lax.all_to_all(grad_couple.reshape(16, 32, 512), LON, 0, 0, tiled=True)
    gathered = jnp.sum(gathered.astype(f32), axis=0)
    table = total_of(messages)

    pieces = jnp.concatenate(
        [
            table[:128].reshape(4, 4, 8, 512).transpose(1, 0, 2, 3).reshape(4, 32, 512),
            table[128:256].reshape(4, 32, 512),
            gathered.reshape(4, 8, 512),
            jnp.broadcast_to(table[256:][None], (4, 64, 512)),
        ],
        axis=1,
    ).astype(bf16)
    rows = [place(pieces, lax.rem(lat + k, 4)) for k in range(4)]
    for k in (1, 2, 3):
        rows[k] = lax.ppermute(rows[k], "lat", ring(4, k))
    mine = total_of(rows).astype(bf16)
    across = lax.ppermute(mine, "zh", ring(2, 1))
    sums = jnp.where(zh == 0, jnp.stack([mine, across]), jnp.stack([across, mine]))
    sums_beside = lax.ppermute(sums, "core", ring(2, 1)).astype(f32)
    sums = sums.astype(f32)
    first = jnp.where(core == 0, sums, sums_beside)
    second = jnp.where(core == 0, sums_beside, sums)
    air = (first[0] + second[0]) + first[1]
    sea_part = second[1]

    def split(total):
        return (
            total[72:128].reshape(7, 8, 512)[:, :7].reshape(49, 512),
            total[128],
            total[:32].reshape(4, 8, 512).transpose(1, 0, 2).reshape(8, 2048),
            total[32:64],
        )

    return (
        (result[None],)
        + split(air)
        + split(sea_part)
        + (air[64:72], sea_part[64:72])
    )


def solution(mesh):
    fine = Mesh(mesh.devices.reshape(2, 2, 4, 4, 4), ("zh", "core", "x", "y", "lat"))
    state = P(COMP, "lat", LON, None)
    rows = P(("x", "y", "lat"), None)
    in_specs = (state, state, P("lat", LON)) + (P(),) * 10
    out_specs = (state, P(), P(), rows, rows, P(), P(), rows, rows, rows, rows)
    return jax.shard_map(
        on_device, mesh=fine, in_specs=in_specs, out_specs=out_specs, check_vma=False
    )
```

```python
import math

import jax
import jax.numpy as jnp
from jax import lax
from jax.experimental import pallas as pl
from jax.experimental.pallas import tpu as pltpu
from jax.sharding import Mesh
from jax.sharding import PartitionSpec as P

tanh_scale = math.sqrt(2.0 / math.pi)
cubic_term = 0.044715
eps_norm = 1e-06
bf16 = jnp.bfloat16
f32 = jnp.float32
PARTS = ((0, 1, 2, 3),)

COMP = ("zh", "core")
LON = ("x", "y")


def ring(count, step):
    return [(i, (i + step) % count) for i in range(count)]


def cross(step, x_core):
    pairs = []
    for c in range(2):
        for x in range(4):
            for y in range(4):
                to = (x, (y + step) % 4) if c != x_core else ((x + step) % 4, y)
                pairs.append((c * 16 + x * 4 + y, c * 16 + to[0] * 4 + to[1]))
    return pairs


def total_of(parts):
    own, one, two, three = [part.astype(f32) for part in parts]
    return (own + two) + (one + three)


def place(parts, index):
    return lax.dynamic_index_in_dim(parts, index, 0, keepdims=False)


def lat_halo(tile):
    north = lax.ppermute(tile[1:4], "lat", [(i, i + 1) for i in range(3)])
    south = lax.ppermute(tile[0:3], "lat", [(i + 1, i) for i in range(3)])
    return north, south


def picker(rows, cols, group, stride):
    row = lax.broadcasted_iota(jnp.int32, (rows, cols), 0)
    col = lax.broadcasted_iota(jnp.int32, (rows, cols), 1)
    pick = lax.rem(row, group) * stride + lax.div(row, group)
    return (pick == col).astype(f32).astype(bf16)


def mm(a, b, dims=((1,), (0,))):
    return lax.dot_general(a, b, (dims, ((), ())), preferred_element_type=f32)


def block_kernel(
    ocean_ref,
    north_ref,
    own_ref,
    south_ref,
    cot_ref,
    mask_ref,
    kern_ref,
    gain_ref,
    w_in_air,
    w_out_air,
    w_in_sea,
    w_out_sea,
    result_ref,
    to_0,
    to_1,
    to_2,
    to_3,
    gct_ref,
    w_in,
    w_out,
    taps_in,
    conv,
    normed,
    norm_in,
    norm_in_t,
    gb,
    branch,
    gnorm,
    small,
    packed,
    out_0,
    out_1,
    out_2,
    out_3,
    sems,
):
    outs = (out_0, out_1, out_2, out_3)
    targets = (to_0, to_1, to_2, to_3)

    def send(j, first, count, sem):
        rows = pl.ds(first, count)
        return pltpu.make_async_copy(outs[j].at[rows], targets[j].at[rows], sems.at[sem])

    here, far_step, near_step = ocean_ref[1], ocean_ref[2], ocean_ref[3]

    def weight_copies(expand, contract):
        copies = []
        for n in range(4):
            a, b = pl.ds(n * 128, 128), pl.ds(n * 512, 512)
            copies.append(pltpu.make_async_copy(expand.at[a], w_in.at[a], sems.at[n]))
            copies.append(pltpu.make_async_copy(contract.at[b], w_out.at[b], sems.at[n + 4]))
        return copies

    @pl.when(ocean_ref[0] == 1)
    def _():
        for copy in weight_copies(w_in_sea, w_out_sea):
            copy.start()

    @pl.when(ocean_ref[0] == 0)
    def _():
        for copy in weight_copies(w_in_air, w_out_air):
            copy.start()

    spread = picker(144, 96, 8, 12)
    for r in range(10):
        src = north_ref[r] if r < 3 else own_ref[r - 3] if r < 7 else south_ref[r - 7]
        q = mm(spread, src)
        for lb in range(4):
            taps_in[lb, r] = q[:, lb * 128 : lb * 128 + 128].reshape(18, 8, 128)
    order = picker(96, 96, 8, 12)
    for i in range(4):
        gb[i * 96 : i * 96 + 96, :] = mm(order, cot_ref[i]).astype(bf16)

    def conv_step(n, carry):
        lb, i = lax.div(n, 4), lax.rem(n, 4)
        acc = [None] * 12
        for u in range(7):
            q = [taps_in[lb, i + u, t] for t in range(18)]
            for v in range(7):
                k = kern_ref[lb, pl.ds(u * 7 + v, 1), :]
                for t in range(12):
                    term = k * q[t + v]
                    acc[t] = term if acc[t] is None else acc[t] + term
        lanes = pl.ds(pl.multiple_of(lb * 128, 128), 128)
        for t in range(12):
            conv[pl.ds(pl.multiple_of(i * 96 + t * 8, 8), 8), lanes] = acc[t]
        return carry

    lax.fori_loop(0, 16, conv_step, 0)

    gain = gain_ref[...]
    scales = []
    for i in range(4):
        rows = slice(i * 96, i * 96 + 96)
        c = conv[rows, :]
        centred = c - jnp.mean(c, axis=1, keepdims=True)
        scale = lax.rsqrt(jnp.mean(centred * centred, axis=1, keepdims=True) + eps_norm)
        z = centred * scale
        scales.append(scale)
        normed[rows, :] = z
        norm_in[rows, :] = (z * gain).astype(bf16)
    turned = norm_in[...].T
    for j in range(16):
        far = lax.rem(lax.div(j, far_step), 4)
        near = lax.rem(lax.div(j, near_step), 4)
        k = lax.rem(far + 4 - here, 4)
        rows = pl.ds(pl.multiple_of(k * 128 + near * 32, 32), 32)
        norm_in_t[rows, :] = turned[j * 32 : j * 32 + 32]
    branch[...] = jnp.zeros_like(branch)
    gnorm[...] = jnp.zeros_like(gnorm)
    for copy in weight_copies(w_in_air, w_out_air):
        copy.wait()

    for k in range(4):
        far = lax.rem(here + k, 4)
        blocks = [far * far_step + near * near_step for near in range(4)]
        picked = [pl.ds(pl.multiple_of(block * 128, 128), 128) for block in blocks]
        for p in PARTS:
            wi = jnp.concatenate([w_in[:, picked[q]] for q in p], axis=1)
            wo = jnp.concatenate([w_out[picked[q], :] for q in p], axis=0)
            pre = mm(norm_in[...], wi)
            square = pre * pre
            half = 0.5 + 0.5 * jnp.tanh(pre * (tanh_scale + (tanh_scale * cubic_term) * square))
            value = pre * half
            hidden = value.astype(bf16)
            slope = half + value * (1.0 - half) * (
                2.0 * tanh_scale + (6.0 * tanh_scale * cubic_term) * square
            )
            gpre = (mm(gb[...], wo, ((1,), (1,))) * slope).astype(bf16)
            branch[...] += mm(hidden, wo)
            gnorm[...] += mm(gpre, wi, ((1,), (1,)))
            gwi = mm(norm_in_t[...], gpre).astype(bf16)
            gwo = mm(hidden, gb[...], ((0,), (0,))).astype(bf16)
            for n, q in enumerate(p):
                lanes = pl.ds(pl.multiple_of(lax.rem(blocks[q], 4) * 128, 128), 128)
                band = lax.div(blocks[q], 4) * 32
                for j in range(4):
                    for near in range(4):
                        rows = pl.ds(pl.multiple_of(near * 256 + band, 32), 32)
                        outs[j][rows, lanes] = gwi[
                            j * 128 + near * 32 : j * 128 + near * 32 + 32,
                            n * 128 : n * 128 + 128,
                        ]
                outs[k][q * 256 + 128 : q * 256 + 256, :] = gwo[n * 128 : n * 128 + 128]
    for j in range(4):
        send(j, 0, 1024, 8 + j).start()

    back = picker(96, 96, 12, 8)
    ggain = jnp.zeros((1, 512), f32)
    for i in range(4):
        rows = slice(i * 96, i * 96 + 96)
        field = jnp.concatenate(
            [taps_in[lb, 3 + i, 3:15].reshape(96, 128) for lb in range(4)], axis=1
        )
        m = mask_ref[rows, :]
        res = (field + jnp.concatenate([m] * 4, axis=1) * branch[rows, :]).astype(bf16)
        result_ref[i] = mm(back, res).astype(bf16)[:90]
        g, z = gnorm[rows, :], normed[rows, :]
        ggain = ggain + jnp.sum(g * z, axis=0, keepdims=True)
        g = g * gain
        conv[rows, :] = scales[i] * (
            g - jnp.mean(g, axis=1, keepdims=True) - z * jnp.mean(g * z, axis=1, keepdims=True)
        )

    to_nat = picker(96, 96, 12, 8)
    to_16 = picker(96, 96, 16, 6)
    shuffle = mm(to_16, to_nat).astype(bf16)
    for i in range(4):
        rows = slice(i * 96, i * 96 + 96)
        moved = mm(shuffle, conv[rows, :].astype(bf16)).astype(bf16)
        norm_in[rows, :] = moved
    gct_ref[...] = norm_in[...].T

    def kern_step(n, carry):
        lb, u = lax.div(n, 7), lax.rem(n, 7)
        lanes = pl.ds(pl.multiple_of(lb * 128, 128), 128)
        acc = [jnp.zeros((8, 128), f32)] * 7
        for i in range(4):
            q = [taps_in[lb, i + u, t] for t in range(18)]
            for t in range(12):
                g = conv[i * 96 + t * 8 : i * 96 + t * 8 + 8, lanes]
                for v in range(7):
                    acc[v] = acc[v] + g * q[t + v]
        rows = [jnp.sum(a, axis=0, keepdims=True) for a in acc] + [jnp.zeros((1, 128), f32)]
        small[pl.ds(pl.multiple_of(u * 8, 8), 8), lanes] = jnp.concatenate(rows, axis=0)
        return carry

    lax.fori_loop(0, 28, kern_step, 0)
    for u in range(7):
        packed[u * 7 : u * 7 + 7, :] = small[u * 8 : u * 8 + 7, :]
    packed[49:50, :] = ggain
    packed[50:64, :] = jnp.zeros((14, 512), f32)
    for out in outs:
        out[1024:1088, :] = packed[...].astype(bf16)
    for j in range(4):
        send(j, 1024, 64, 12 + j).start()
    for j in range(4):
        send(j, 0, 1024, 8 + j).wait()
        send(j, 1024, 64, 12 + j).wait()


def block(ocean, north, own, south, cot, mask, kern, gain, wia, woa, wis, wos):
    vmem = pl.BlockSpec(memory_space=pltpu.VMEM)
    hbm = pl.BlockSpec(memory_space=pl.ANY)
    flops = 2 * 6 * 384 * 512 * 2048
    return pl.pallas_call(
        block_kernel,
        out_shape=(
            jax.ShapeDtypeStruct((4, 90, 512), bf16),
            *[jax.ShapeDtypeStruct((1088, 512), bf16)] * 4,
            jax.ShapeDtypeStruct((512, 384), bf16),
        ),
        in_specs=[pl.BlockSpec(memory_space=pltpu.SMEM)] + [vmem] * 7 + [hbm] * 4,
        out_specs=(vmem,) + (hbm,) * 4 + (vmem,),
        scratch_shapes=[
            pltpu.VMEM((512, 2048), bf16),
            pltpu.VMEM((2048, 512), bf16),
            pltpu.VMEM((4, 10, 18, 8, 128), f32),
            pltpu.VMEM((384, 512), f32),
            pltpu.VMEM((384, 512), f32),
            pltpu.VMEM((384, 512), bf16),
            pltpu.VMEM((512, 384), bf16),
            pltpu.VMEM((384, 512), bf16),
            pltpu.VMEM((384, 512), f32),
            pltpu.VMEM((384, 512), f32),
            pltpu.VMEM((56, 512), f32),
            pltpu.VMEM((64, 512), f32),
            *[pltpu.VMEM((1088, 512), bf16)] * 4,
            pltpu.SemaphoreType.DMA((16,)),
        ],
        compiler_params=pltpu.CompilerParams(vmem_limit_bytes=56 * 1024 * 1024),
        cost_estimate=pl.CostEstimate(
            flops=flops, bytes_accessed=12 * 1024 * 1024, transcendentals=384 * 2048
        ),
        name="block_kernel",
    )(ocean, north, own, south, cot, mask, kern, gain, wia, woa, wis, wos)


def couple_kernel(
    north_ref, own_ref, south_ref, gct_ref, cot_ref, kern_ref, scale_ref, out_ref, rows16, acc, gct, taps
):
    spread = picker(192, 96, 16, 6)
    for r in range(10):
        src = north_ref[r] if r < 3 else own_ref[r - 3] if r < 7 else south_ref[r - 7]
        rows16[r] = mm(spread, src).astype(bf16)
    order = picker(96, 96, 16, 6)
    moved = [mm(order, cot_ref[i]).astype(bf16) for i in range(4)]
    acc[...] = mm(jnp.concatenate(moved, axis=0).T, rows16[3:7, 48:144, :].reshape(384, 512))
    gct[...] = gct_ref[...].astype(f32)
    turned = kern_ref[...].T
    for u in range(7):
        taps[u] = turned[:, u * 8 : u * 8 + 8]

    def step(u, carry):
        left, right = [], []
        for v in range(7):
            left.append((taps[u, :, v : v + 1] * gct[...]).astype(bf16))
            right.append(rows16[pl.ds(u, 4), v * 16 : v * 16 + 96, :].reshape(384, 512))
        acc[...] += mm(jnp.concatenate(left, axis=1), jnp.concatenate(right, axis=0))
        return carry

    lax.fori_loop(0, 7, step, 0)
    out_ref[...] = (acc[...] * scale_ref[0]).astype(bf16).T


def couple(north, own, south, gct, cot, kern, scale):
    vmem = pl.BlockSpec(memory_space=pltpu.VMEM)
    return pl.pallas_call(
        couple_kernel,
        out_shape=jax.ShapeDtypeStruct((512, 512), bf16),
        in_specs=[vmem] * 6 + [pl.BlockSpec(memory_space=pltpu.SMEM)],
        out_specs=vmem,
        scratch_shapes=[
            pltpu.VMEM((10, 192, 512), bf16),
            pltpu.VMEM((512, 512), f32),
            pltpu.VMEM((512, 384), f32),
            pltpu.VMEM((7, 512, 8), f32),
        ],
        compiler_params=pltpu.CompilerParams(vmem_limit_bytes=24 * 1024 * 1024),
        cost_estimate=pl.CostEstimate(
            flops=2 * 50 * 384 * 512 * 512, bytes_accessed=4 * 1024 * 1024, transcendentals=0
        ),
        name="couple_kernel",
    )(north, own, south, gct, cot, kern, scale)


def finish_kernel(place_ref, mine_ref, mine_beside_ref, across_ref, across_beside_ref, *refs):
    outs, total = refs[:10], refs[10]
    first_zh, first_core = place_ref[0] == 0, place_ref[1] == 0
    mine, across = mine_ref[...].astype(f32), across_ref[...].astype(f32)
    mine_beside = mine_beside_ref[...].astype(f32)
    across_beside = across_beside_ref[...].astype(f32)
    near = jnp.where(first_zh, mine, across)
    near_beside = jnp.where(first_zh, mine_beside, across_beside)
    far = jnp.where(first_zh, across, mine)
    far_beside = jnp.where(first_zh, across_beside, mine_beside)
    far_air = jnp.where(first_core, far, far_beside)
    total[0] = (near + near_beside) + far_air
    total[1] = jnp.where(first_core, far_beside, far)
    for n in range(2):
        kern_ref, gain_ref, expand_ref, contract_ref = outs[n * 4 : n * 4 + 4]
        kern_ref[...] = total[n, 72:121, :]
        gain_ref[...] = total[n, 121:122, :]
        for cb in range(4):
            expand_ref[:, cb * 512 : cb * 512 + 512] = total[n, cb * 8 : cb * 8 + 8, :]
        contract_ref[...] = total[n, 32:64, :]
        outs[8 + n][...] = total[n, 64:72, :]


def finish(here, mine, mine_beside, across, across_beside):
    vmem = pl.BlockSpec(memory_space=pltpu.VMEM)
    shapes = [(49, 512), (1, 512), (8, 2048), (32, 512)] * 2 + [(8, 512)] * 2
    return pl.pallas_call(
        finish_kernel,
        out_shape=[jax.ShapeDtypeStruct(shape, f32) for shape in shapes],
        in_specs=[pl.BlockSpec(memory_space=pltpu.SMEM)] + [vmem] * 4,
        out_specs=[vmem] * 10,
        scratch_shapes=[pltpu.VMEM((2, 128, 512), f32)],
        compiler_params=pltpu.CompilerParams(vmem_limit_bytes=8 * 1024 * 1024),
        name="finish_kernel",
    )(here, mine, mine_beside, across, across_beside)


def on_device(
    component_snapshots,
    cotangent,
    land,
    atmosphere_kernel,
    atmosphere_gain,
    atmosphere_expand_weight,
    atmosphere_contract_weight,
    ocean_kernel,
    ocean_gain,
    ocean_expand_weight,
    ocean_contract_weight,
    marine_to_air_map,
    flux_weight,
):
    zh, core = lax.axis_index("zh"), lax.axis_index("core")
    is_ocean = (zh == 1) & (core == 1)
    copies = 3.0
    sea = (1 - land).astype(f32)
    local = component_snapshots[0]

    def edge(columns):
        flags = jnp.broadcast_to(sea[:, columns].astype(bf16)[:, :, None], (4, 3, 128))
        return jnp.concatenate([local[:, columns], flags], axis=2)

    west = lax.ppermute(edge(slice(87, 90)), LON, ring(16, 1))
    east = lax.ppermute(edge(slice(0, 3)), LON, ring(16, -1))
    local = jnp.concatenate([west[:, :, :512], local, east[:, :, :512]], axis=1)
    sea_wide = jnp.concatenate(
        [west[:, :, 512].astype(f32), sea, east[:, :, 512].astype(f32)], axis=1
    )

    beside = lax.ppermute(local, "core", ring(2, 1))
    pair_sum = (local.astype(f32) + beside.astype(f32)).astype(bf16)
    payload = jnp.where(zh == 0, pair_sum, jnp.where(core == 0, beside, local))
    half = lax.dynamic_slice_in_dim(payload, core * 2, 2, axis=0)
    got = lax.ppermute(half, "zh", ring(2, 1))
    coupling = jnp.where(is_ocean, flux_weight, marine_to_air_map)
    kernel = jnp.where(is_ocean, ocean_kernel, atmosphere_kernel)
    gain = jnp.where(is_ocean, ocean_gain, atmosphere_gain)
    mask = jnp.where(is_ocean, sea, jnp.ones_like(sea))
    grad_branch = (mask[:, :, None] * cotangent[0].astype(f32)).astype(bf16)
    grad_branch = jnp.pad(grad_branch, ((0, 0), (0, 6), (0, 0)))
    mask = jnp.pad(mask, ((0, 0), (0, 6))).reshape(4, 8, 12).transpose(0, 2, 1).reshape(384, 1)
    mask = jnp.broadcast_to(mask, (384, 128))
    kernel_lanes = kernel.reshape(49, 4, 128).transpose(1, 0, 2)
    kernel_rows = jnp.pad(kernel.reshape(7, 7, 512), ((0, 1), (0, 1), (0, 0))).reshape(64, 512)
    got, coupling, kernel_lanes, kernel_rows, gain, mask, grad_branch = lax.optimization_barrier(
        (got, coupling, kernel_lanes, kernel_rows, gain, mask, grad_branch)
    )
    got_beside = lax.ppermute(got, "core", ring(2, 1))
    full = jnp.where(
        core == 0,
        jnp.concatenate([got, got_beside], axis=0),
        jnp.concatenate([got_beside, got], axis=0),
    )
    ocean_sum = (full.astype(f32) + beside.astype(f32)).astype(bf16)
    partner = jnp.where(zh == 0, full, jnp.where(core == 0, beside, ocean_sum))

    projected = jnp.dot(partner.reshape(384, 512), coupling, preferred_element_type=f32)
    forcing = jnp.where(is_ocean, projected / copies, projected.astype(bf16).astype(f32))
    field = local.astype(f32) + sea_wide[:, :, None] * forcing.reshape(4, 96, 512)
    field = field.astype(bf16)
    north, south = lat_halo(field)
    masked = (sea_wide[:, :, None] * partner.astype(f32)).astype(bf16)
    masked_north, masked_south = lat_halo(masked)

    x, y, lat = (lax.axis_index(axis) for axis in ("x", "y", "lat"))
    result, *parts, grad_conv_t = block(
        jnp.stack(
            [
                is_ocean.astype(jnp.int32),
                jnp.where(core == 0, x, y),
                jnp.where(core == 0, 4, 1),
                jnp.where(core == 0, 1, 4),
            ]
        ),
        north,
        field,
        south,
        grad_branch,
        mask,
        kernel_lanes,
        gain[None],
        atmosphere_expand_weight,
        atmosphere_contract_weight,
        ocean_expand_weight,
        ocean_contract_weight,
    )

    for k in (1, 2, 3):
        parts[k] = lax.ppermute(parts[k], ("core", "x", "y"), cross(k, 0))

    grad_couple = couple(
        masked_north,
        masked,
        masked_south,
        grad_conv_t,
        grad_branch,
        kernel_rows,
        jnp.where(is_ocean, 1.0 / copies, 1.0).astype(f32).reshape(1),
    )
    small = total_of([part[1024:1080] for part in parts])
    near = jnp.where(core == 0, y, x)
    messages = []
    for k in range(4):
        start = lax.rem(near + k, 4) * 256
        table = total_of([lax.dynamic_slice_in_dim(part, start, 256, 0) for part in parts])
        messages.append(jnp.concatenate([table, small], axis=0).astype(bf16))
    for k in (1, 2, 3):
        messages[k] = lax.ppermute(messages[k], ("core", "x", "y"), cross(k, 1))
    gathered = lax.all_to_all(grad_couple.reshape(16, 32, 512), LON, 0, 0, tiled=True)
    result, gathered = lax.optimization_barrier((result[None], gathered))
    gathered = jnp.sum(gathered.astype(f32), axis=0)
    table = total_of(messages)

    pieces = jnp.concatenate(
        [
            table[:128].reshape(4, 4, 8, 512).transpose(1, 0, 2, 3).reshape(4, 32, 512),
            table[128:256].reshape(4, 32, 512),
            gathered.reshape(4, 8, 512),
            jnp.broadcast_to(table[256:][None], (4, 56, 512)),
        ],
        axis=1,
    ).astype(bf16)
    rows = [place(pieces, lax.rem(lat + k, 4)) for k in range(4)]
    for k in (1, 2, 3):
        rows[k] = lax.ppermute(rows[k], "lat", ring(4, k))
    mine = total_of(rows).astype(bf16)
    mine_beside = lax.ppermute(mine, "core", ring(2, 1))
    across = lax.ppermute(mine, "zh", ring(2, 1))
    across_beside = lax.ppermute(across, "core", ring(2, 1))
    outs = finish(jnp.stack([zh, core]), mine, mine_beside, across, across_beside)
    return (
        (result,)
        + (outs[0], outs[1].reshape(512), outs[2], outs[3])
        + (outs[4], outs[5].reshape(512), outs[6], outs[7])
        + (outs[8], outs[9])
    )


def solution(mesh):
    fine = Mesh(mesh.devices.reshape(2, 2, 4, 4, 4), ("zh", "core", "x", "y", "lat"))
    state = P(COMP, "lat", LON, None)
    rows = P(("x", "y", "lat"), None)
    in_specs = (state, state, P("lat", LON)) + (P(),) * 10
    out_specs = (state, P(), P(), rows, rows, P(), P(), rows, rows, rows, rows)
    return jax.shard_map(
        on_device, mesh=fine, in_specs=in_specs, out_specs=out_specs, check_vma=False
    )
```

```python
import math

import jax
import jax.numpy as jnp
from jax import lax
from jax.experimental import pallas as pl
from jax.experimental.pallas import tpu as pltpu
from jax.sharding import Mesh
from jax.sharding import PartitionSpec as P

tanh_scale = math.sqrt(2.0 / math.pi)
cubic_term = 0.044715
eps_norm = 1e-06
bf16 = jnp.bfloat16
f32 = jnp.float32
PARTS = ((0, 1, 2, 3),)

COMP = ("zh", "core")
LON = ("x", "y")


def ring(count, step):
    return [(i, (i + step) % count) for i in range(count)]


def cross(step, x_core):
    pairs = []
    for c in range(2):
        for x in range(4):
            for y in range(4):
                to = (x, (y + step) % 4) if c != x_core else ((x + step) % 4, y)
                pairs.append((c * 16 + x * 4 + y, c * 16 + to[0] * 4 + to[1]))
    return pairs


def total_of(parts):
    own, one, two, three = [part.astype(f32) for part in parts]
    return (own + two) + (one + three)


def place(parts, index):
    return lax.dynamic_index_in_dim(parts, index, 0, keepdims=False)


def lat_halo(tile):
    north = lax.ppermute(tile[1:4], "lat", [(i, i + 1) for i in range(3)])
    south = lax.ppermute(tile[0:3], "lat", [(i + 1, i) for i in range(3)])
    return north, south


def picker(rows, cols, group, stride):
    row = lax.broadcasted_iota(jnp.int32, (rows, cols), 0)
    col = lax.broadcasted_iota(jnp.int32, (rows, cols), 1)
    pick = lax.rem(row, group) * stride + lax.div(row, group)
    return (pick == col).astype(f32).astype(bf16)


def mm(a, b, dims=((1,), (0,))):
    return lax.dot_general(a, b, (dims, ((), ())), preferred_element_type=f32)


def block_kernel(
    ocean_ref,
    north_ref,
    own_ref,
    south_ref,
    cot_ref,
    mask_ref,
    kern_ref,
    gain_ref,
    w_in_air,
    w_out_air,
    w_in_sea,
    w_out_sea,
    result_ref,
    to_0,
    to_1,
    to_2,
    to_3,
    gct_ref,
    w_in,
    w_out,
    taps_in,
    conv,
    normed,
    norm_in,
    norm_in_t,
    gb,
    branch,
    gnorm,
    small,
    packed,
    out_0,
    out_1,
    out_2,
    out_3,
    sems,
):
    outs = (out_0, out_1, out_2, out_3)
    targets = (to_0, to_1, to_2, to_3)

    def send(j, first, count, sem):
        rows = pl.ds(first, count)
        return pltpu.make_async_copy(outs[j].at[rows], targets[j].at[rows], sems.at[sem])

    here, far_step, near_step = ocean_ref[1], ocean_ref[2], ocean_ref[3]

    def weight_copies(expand, contract):
        copies = []
        for n in range(4):
            a, b = pl.ds(n * 128, 128), pl.ds(n * 512, 512)
            copies.append(pltpu.make_async_copy(expand.at[a], w_in.at[a], sems.at[n]))
            copies.append(pltpu.make_async_copy(contract.at[b], w_out.at[b], sems.at[n + 4]))
        return copies

    @pl.when(ocean_ref[0] == 1)
    def _():
        for copy in weight_copies(w_in_sea, w_out_sea):
            copy.start()

    @pl.when(ocean_ref[0] == 0)
    def _():
        for copy in weight_copies(w_in_air, w_out_air):
            copy.start()

    spread = picker(144, 96, 8, 12)
    for r in range(10):
        src = north_ref[r] if r < 3 else own_ref[r - 3] if r < 7 else south_ref[r - 7]
        q = mm(spread, src)
        for lb in range(4):
            taps_in[lb, r] = q[:, lb * 128 : lb * 128 + 128].reshape(18, 8, 128)
    order = picker(96, 96, 8, 12)
    for i in range(4):
        gb[i * 96 : i * 96 + 96, :] = mm(order, cot_ref[i]).astype(bf16)

    def conv_step(n, carry):
        lb, i = lax.div(n, 4), lax.rem(n, 4)
        acc = [None] * 12
        for u in range(7):
            q = [taps_in[lb, i + u, t] for t in range(18)]
            for v in range(7):
                k = kern_ref[lb, pl.ds(u * 7 + v, 1), :]
                for t in range(12):
                    term = k * q[t + v]
                    acc[t] = term if acc[t] is None else acc[t] + term
        lanes = pl.ds(pl.multiple_of(lb * 128, 128), 128)
        for t in range(12):
            conv[pl.ds(pl.multiple_of(i * 96 + t * 8, 8), 8), lanes] = acc[t]
        return carry

    lax.fori_loop(0, 16, conv_step, 0)

    gain = gain_ref[...]
    scales = []
    for i in range(4):
        rows = slice(i * 96, i * 96 + 96)
        c = conv[rows, :]
        centred = c - jnp.mean(c, axis=1, keepdims=True)
        scale = lax.rsqrt(jnp.mean(centred * centred, axis=1, keepdims=True) + eps_norm)
        z = centred * scale
        scales.append(scale)
        normed[rows, :] = z
        norm_in[rows, :] = (z * gain).astype(bf16)
    turned = norm_in[...].T
    for j in range(16):
        far = lax.rem(lax.div(j, far_step), 4)
        near = lax.rem(lax.div(j, near_step), 4)
        k = lax.rem(far + 4 - here, 4)
        rows = pl.ds(pl.multiple_of(k * 128 + near * 32, 32), 32)
        norm_in_t[rows, :] = turned[j * 32 : j * 32 + 32]
    branch[...] = jnp.zeros_like(branch)
    gnorm[...] = jnp.zeros_like(gnorm)
    for copy in weight_copies(w_in_air, w_out_air):
        copy.wait()

    for k in range(4):
        far = lax.rem(here + k, 4)
        blocks = [far * far_step + near * near_step for near in range(4)]
        picked = [pl.ds(pl.multiple_of(block * 128, 128), 128) for block in blocks]
        for p in PARTS:
            wi = jnp.concatenate([w_in[:, picked[q]] for q in p], axis=1)
            wo = jnp.concatenate([w_out[picked[q], :] for q in p], axis=0)
            pre = mm(norm_in[...], wi)
            square = pre * pre
            half = 0.5 + 0.5 * jnp.tanh(pre * (tanh_scale + (tanh_scale * cubic_term) * square))
            value = pre * half
            hidden = value.astype(bf16)
            slope = half + value * (1.0 - half) * (
                2.0 * tanh_scale + (6.0 * tanh_scale * cubic_term) * square
            )
            gpre = (mm(gb[...], wo, ((1,), (1,))) * slope).astype(bf16)
            branch[...] += mm(hidden, wo)
            gnorm[...] += mm(gpre, wi, ((1,), (1,)))
            gwi = mm(norm_in_t[...], gpre).astype(bf16)
            gwo = mm(hidden, gb[...], ((0,), (0,))).astype(bf16)
            for n, q in enumerate(p):
                lanes = pl.ds(pl.multiple_of(lax.rem(blocks[q], 4) * 128, 128), 128)
                band = lax.div(blocks[q], 4) * 32
                for j in range(4):
                    for near in range(4):
                        rows = pl.ds(pl.multiple_of(near * 256 + band, 32), 32)
                        outs[j][rows, lanes] = gwi[
                            j * 128 + near * 32 : j * 128 + near * 32 + 32,
                            n * 128 : n * 128 + 128,
                        ]
                outs[k][q * 256 + 128 : q * 256 + 256, :] = gwo[n * 128 : n * 128 + 128]
    for j in range(4):
        send(j, 0, 1024, 8 + j).start()

    back = picker(96, 96, 12, 8)
    ggain = jnp.zeros((1, 512), f32)
    for i in range(4):
        rows = slice(i * 96, i * 96 + 96)
        field = jnp.concatenate(
            [taps_in[lb, 3 + i, 3:15].reshape(96, 128) for lb in range(4)], axis=1
        )
        m = mask_ref[rows, :]
        res = (field + jnp.concatenate([m] * 4, axis=1) * branch[rows, :]).astype(bf16)
        result_ref[i] = mm(back, res).astype(bf16)[:90]
        g, z = gnorm[rows, :], normed[rows, :]
        ggain = ggain + jnp.sum(g * z, axis=0, keepdims=True)
        g = g * gain
        conv[rows, :] = scales[i] * (
            g - jnp.mean(g, axis=1, keepdims=True) - z * jnp.mean(g * z, axis=1, keepdims=True)
        )

    to_nat = picker(96, 96, 12, 8)
    to_16 = picker(96, 96, 16, 6)
    shuffle = mm(to_16, to_nat).astype(bf16)
    for i in range(4):
        rows = slice(i * 96, i * 96 + 96)
        moved = mm(shuffle, conv[rows, :].astype(bf16)).astype(bf16)
        norm_in[rows, :] = moved
    gct_ref[...] = norm_in[...].T

    def kern_step(n, carry):
        lb, u = lax.div(n, 7), lax.rem(n, 7)
        lanes = pl.ds(pl.multiple_of(lb * 128, 128), 128)
        acc = [jnp.zeros((8, 128), f32)] * 7
        for i in range(4):
            q = [taps_in[lb, i + u, t] for t in range(18)]
            for t in range(12):
                g = conv[i * 96 + t * 8 : i * 96 + t * 8 + 8, lanes]
                for v in range(7):
                    acc[v] = acc[v] + g * q[t + v]
        rows = [jnp.sum(a, axis=0, keepdims=True) for a in acc] + [jnp.zeros((1, 128), f32)]
        small[pl.ds(pl.multiple_of(u * 8, 8), 8), lanes] = jnp.concatenate(rows, axis=0)
        return carry

    lax.fori_loop(0, 28, kern_step, 0)
    for u in range(7):
        packed[u * 7 : u * 7 + 7, :] = small[u * 8 : u * 8 + 7, :]
    packed[49:50, :] = ggain
    packed[50:64, :] = jnp.zeros((14, 512), f32)
    for out in outs:
        out[1024:1088, :] = packed[...].astype(bf16)
    for j in range(4):
        send(j, 1024, 64, 12 + j).start()
    for j in range(4):
        send(j, 0, 1024, 8 + j).wait()
        send(j, 1024, 64, 12 + j).wait()


def block(ocean, north, own, south, cot, mask, kern, gain, wia, woa, wis, wos):
    vmem = pl.BlockSpec(memory_space=pltpu.VMEM)
    hbm = pl.BlockSpec(memory_space=pltpu.HBM)
    flops = 2 * 6 * 384 * 512 * 2048
    return pl.pallas_call(
        block_kernel,
        out_shape=(
            jax.ShapeDtypeStruct((4, 90, 512), bf16),
            *[jax.ShapeDtypeStruct((1088, 512), bf16)] * 4,
            jax.ShapeDtypeStruct((512, 384), bf16),
        ),
        in_specs=[pl.BlockSpec(memory_space=pltpu.SMEM)] + [vmem] * 7 + [hbm] * 4,
        out_specs=(vmem,) + (hbm,) * 4 + (vmem,),
        scratch_shapes=[
            pltpu.VMEM((512, 2048), bf16),
            pltpu.VMEM((2048, 512), bf16),
            pltpu.VMEM((4, 10, 18, 8, 128), f32),
            pltpu.VMEM((384, 512), f32),
            pltpu.VMEM((384, 512), f32),
            pltpu.VMEM((384, 512), bf16),
            pltpu.VMEM((512, 384), bf16),
            pltpu.VMEM((384, 512), bf16),
            pltpu.VMEM((384, 512), f32),
            pltpu.VMEM((384, 512), f32),
            pltpu.VMEM((56, 512), f32),
            pltpu.VMEM((64, 512), f32),
            *[pltpu.VMEM((1088, 512), bf16)] * 4,
            pltpu.SemaphoreType.DMA((16,)),
        ],
        compiler_params=pltpu.CompilerParams(vmem_limit_bytes=40 * 1024 * 1024),
        cost_estimate=pl.CostEstimate(
            flops=flops, bytes_accessed=12 * 1024 * 1024, transcendentals=384 * 2048
        ),
        name="block_kernel",
    )(ocean, north, own, south, cot, mask, kern, gain, wia, woa, wis, wos)


def couple_kernel(
    north_ref, own_ref, south_ref, gct_ref, cot_ref, kern_ref, scale_ref, out_ref, rows16, acc, gct, taps
):
    spread = picker(192, 96, 16, 6)
    for r in range(10):
        src = north_ref[r] if r < 3 else own_ref[r - 3] if r < 7 else south_ref[r - 7]
        rows16[r] = mm(spread, src).astype(bf16)
    order = picker(96, 96, 16, 6)
    moved = [mm(order, cot_ref[i]).astype(bf16) for i in range(4)]
    acc[...] = mm(jnp.concatenate(moved, axis=0).T, rows16[3:7, 48:144, :].reshape(384, 512))
    gct[...] = gct_ref[...].astype(f32)
    turned = kern_ref[...].T
    for u in range(7):
        taps[u] = turned[:, u * 8 : u * 8 + 8]

    def step(u, carry):
        left, right = [], []
        for v in range(7):
            left.append((taps[u, :, v : v + 1] * gct[...]).astype(bf16))
            right.append(rows16[pl.ds(u, 4), v * 16 : v * 16 + 96, :].reshape(384, 512))
        acc[...] += mm(jnp.concatenate(left, axis=1), jnp.concatenate(right, axis=0))
        return carry

    lax.fori_loop(0, 7, step, 0)
    out_ref[...] = (acc[...] * scale_ref[0]).astype(bf16).T


def couple(north, own, south, gct, cot, kern, scale):
    vmem = pl.BlockSpec(memory_space=pltpu.VMEM)
    return pl.pallas_call(
        couple_kernel,
        out_shape=jax.ShapeDtypeStruct((512, 512), bf16),
        in_specs=[vmem] * 6 + [pl.BlockSpec(memory_space=pltpu.SMEM)],
        out_specs=vmem,
        scratch_shapes=[
            pltpu.VMEM((10, 192, 512), bf16),
            pltpu.VMEM((512, 512), f32),
            pltpu.VMEM((512, 384), f32),
            pltpu.VMEM((7, 512, 8), f32),
        ],
        compiler_params=pltpu.CompilerParams(vmem_limit_bytes=24 * 1024 * 1024),
        cost_estimate=pl.CostEstimate(
            flops=2 * 50 * 384 * 512 * 512, bytes_accessed=4 * 1024 * 1024, transcendentals=0
        ),
        name="couple_kernel",
    )(north, own, south, gct, cot, kern, scale)


def finish_kernel(place_ref, mine_ref, mine_beside_ref, across_ref, across_beside_ref, *refs):
    outs, total = refs[:10], refs[10]
    first_zh, first_core = place_ref[0] == 0, place_ref[1] == 0
    mine, across = mine_ref[...].astype(f32), across_ref[...].astype(f32)
    mine_beside = mine_beside_ref[...].astype(f32)
    across_beside = across_beside_ref[...].astype(f32)
    near = jnp.where(first_zh, mine, across)
    near_beside = jnp.where(first_zh, mine_beside, across_beside)
    far = jnp.where(first_zh, across, mine)
    far_beside = jnp.where(first_zh, across_beside, mine_beside)
    far_air = jnp.where(first_core, far, far_beside)
    total[0] = (near + near_beside) + far_air
    total[1] = jnp.where(first_core, far_beside, far)
    for n in range(2):
        kern_ref, gain_ref, expand_ref, contract_ref = outs[n * 4 : n * 4 + 4]
        kern_ref[...] = total[n, 64:113, :]
        gain_ref[...] = total[n, 113:114, :]
        for cb in range(4):
            expand_ref[:, cb * 512 : cb * 512 + 512] = total[n, cb * 8 : cb * 8 + 8, :]
        contract_ref[...] = total[n, 32:64, :]
        outs[8 + n][...] = total[n, 120:128, :]


def finish(here, mine, mine_beside, across, across_beside):
    vmem = pl.BlockSpec(memory_space=pltpu.VMEM)
    shapes = [(49, 512), (1, 512), (8, 2048), (32, 512)] * 2 + [(8, 512)] * 2
    return pl.pallas_call(
        finish_kernel,
        out_shape=[jax.ShapeDtypeStruct(shape, f32) for shape in shapes],
        in_specs=[pl.BlockSpec(memory_space=pltpu.SMEM)] + [vmem] * 4,
        out_specs=[vmem] * 10,
        scratch_shapes=[pltpu.VMEM((2, 128, 512), f32)],
        compiler_params=pltpu.CompilerParams(vmem_limit_bytes=8 * 1024 * 1024),
        name="finish_kernel",
    )(here, mine, mine_beside, across, across_beside)


def on_device(
    component_snapshots,
    cotangent,
    land,
    atmosphere_kernel,
    atmosphere_gain,
    atmosphere_expand_weight,
    atmosphere_contract_weight,
    ocean_kernel,
    ocean_gain,
    ocean_expand_weight,
    ocean_contract_weight,
    marine_to_air_map,
    flux_weight,
):
    zh, core = lax.axis_index("zh"), lax.axis_index("core")
    is_ocean = (zh == 1) & (core == 1)
    copies = 3.0
    sea = (1 - land).astype(f32)
    local = component_snapshots[0]

    def edge(columns):
        flags = jnp.broadcast_to(sea[:, columns].astype(bf16)[:, :, None], (4, 3, 128))
        return jnp.concatenate([local[:, columns], flags], axis=2)

    west = lax.ppermute(edge(slice(87, 90)), LON, ring(16, 1))
    east = lax.ppermute(edge(slice(0, 3)), LON, ring(16, -1))
    local = jnp.concatenate([west[:, :, :512], local, east[:, :, :512]], axis=1)
    sea_wide = jnp.concatenate(
        [west[:, :, 512].astype(f32), sea, east[:, :, 512].astype(f32)], axis=1
    )

    beside = lax.ppermute(local, "core", ring(2, 1))
    pair_sum = (local.astype(f32) + beside.astype(f32)).astype(bf16)
    payload = jnp.where(zh == 0, pair_sum, jnp.where(core == 0, beside, local))
    half = lax.dynamic_slice_in_dim(payload, core * 2, 2, axis=0)
    got = lax.ppermute(half, "zh", ring(2, 1))
    coupling = jnp.where(is_ocean, flux_weight, marine_to_air_map)
    kernel = jnp.where(is_ocean, ocean_kernel, atmosphere_kernel)
    gain = jnp.where(is_ocean, ocean_gain, atmosphere_gain)
    mask = jnp.where(is_ocean, sea, jnp.ones_like(sea))
    grad_branch = (mask[:, :, None] * cotangent[0].astype(f32)).astype(bf16)
    grad_branch = jnp.pad(grad_branch, ((0, 0), (0, 6), (0, 0)))
    mask = jnp.pad(mask, ((0, 0), (0, 6))).reshape(4, 8, 12).transpose(0, 2, 1).reshape(384, 1)
    mask = jnp.broadcast_to(mask, (384, 128))
    kernel_lanes = kernel.reshape(49, 4, 128).transpose(1, 0, 2)
    kernel_rows = jnp.pad(kernel.reshape(7, 7, 512), ((0, 1), (0, 1), (0, 0))).reshape(64, 512)
    got, coupling, kernel_lanes, kernel_rows, gain, mask, grad_branch = lax.optimization_barrier(
        (got, coupling, kernel_lanes, kernel_rows, gain, mask, grad_branch)
    )
    got_beside = lax.ppermute(got, "core", ring(2, 1))
    full = jnp.where(
        core == 0,
        jnp.concatenate([got, got_beside], axis=0),
        jnp.concatenate([got_beside, got], axis=0),
    )
    ocean_sum = (full.astype(f32) + beside.astype(f32)).astype(bf16)
    partner = jnp.where(zh == 0, full, jnp.where(core == 0, beside, ocean_sum))

    projected = jnp.dot(partner.reshape(384, 512), coupling, preferred_element_type=f32)
    forcing = jnp.where(is_ocean, projected / copies, projected.astype(bf16).astype(f32))
    field = local.astype(f32) + sea_wide[:, :, None] * forcing.reshape(4, 96, 512)
    field = field.astype(bf16)
    north, south = lat_halo(field)
    masked = (sea_wide[:, :, None] * partner.astype(f32)).astype(bf16)
    masked_north, masked_south = lat_halo(masked)

    x, y, lat = (lax.axis_index(axis) for axis in ("x", "y", "lat"))
    result, *parts, grad_conv_t = block(
        jnp.stack(
            [
                is_ocean.astype(jnp.int32),
                jnp.where(core == 0, x, y),
                jnp.where(core == 0, 4, 1),
                jnp.where(core == 0, 1, 4),
            ]
        ),
        north,
        field,
        south,
        grad_branch,
        mask,
        kernel_lanes,
        gain[None],
        atmosphere_expand_weight,
        atmosphere_contract_weight,
        ocean_expand_weight,
        ocean_contract_weight,
    )

    for k in (1, 2, 3):
        parts[k] = lax.ppermute(parts[k], ("core", "x", "y"), cross(k, 0))

    grad_couple = couple(
        masked_north,
        masked,
        masked_south,
        grad_conv_t,
        grad_branch,
        kernel_rows,
        jnp.where(is_ocean, 1.0 / copies, 1.0).astype(f32).reshape(1),
    )
    small = total_of([part[1024:1080] for part in parts])
    near = jnp.where(core == 0, y, x)
    messages = []
    for k in range(4):
        start = lax.rem(near + k, 4) * 256
        table = total_of([lax.dynamic_slice_in_dim(part, start, 256, 0) for part in parts])
        messages.append(jnp.concatenate([table, small], axis=0).astype(bf16))
    for k in (1, 2, 3):
        messages[k] = lax.ppermute(messages[k], ("core", "x", "y"), cross(k, 1))
    shares = grad_couple.reshape(16, 4, 8, 512)
    shares = [
        lax.dynamic_index_in_dim(shares, lax.rem(lat + k, 4), 1, keepdims=False) for k in range(4)
    ]
    for k in (1, 2, 3):
        shares[k] = lax.ppermute(shares[k], "lat", ring(4, k))
    gathered = lax.all_to_all(total_of(shares).astype(bf16), LON, 0, 0, tiled=True)
    gathered = jnp.sum(gathered.astype(f32), axis=0)
    table = total_of(messages)

    pieces = jnp.concatenate(
        [
            table[:128].reshape(4, 4, 8, 512).transpose(1, 0, 2, 3).reshape(4, 32, 512),
            table[128:256].reshape(4, 32, 512),
            jnp.broadcast_to(table[256:][None], (4, 56, 512)),
        ],
        axis=1,
    ).astype(bf16)
    rows = [place(pieces, lax.rem(lat + k, 4)) for k in range(4)]
    for k in (1, 2, 3):
        rows[k] = lax.ppermute(rows[k], "lat", ring(4, k))
    mine = jnp.concatenate([total_of(rows), gathered], axis=0).astype(bf16)
    mine_beside = lax.ppermute(mine, "core", ring(2, 1))
    across = lax.ppermute(mine, "zh", ring(2, 1))
    across_beside = lax.ppermute(across, "core", ring(2, 1))
    outs = finish(jnp.stack([zh, core]), mine, mine_beside, across, across_beside)
    return (
        (result[None],)
        + (outs[0], outs[1].reshape(512), outs[2], outs[3])
        + (outs[4], outs[5].reshape(512), outs[6], outs[7])
        + (outs[8], outs[9])
    )


def solution(mesh):
    fine = Mesh(mesh.devices.reshape(2, 2, 4, 4, 4), ("zh", "core", "x", "y", "lat"))
    state = P(COMP, "lat", LON, None)
    rows = P(("x", "y", "lat"), None)
    in_specs = (state, state, P("lat", LON)) + (P(),) * 10
    out_specs = (state, P(), P(), rows, rows, P(), P(), rows, rows, rows, rows)
    return jax.shard_map(
        on_device, mesh=fine, in_specs=in_specs, out_specs=out_specs, check_vma=False
    )
```

```python
import math

import jax
import jax.numpy as jnp
from jax import lax
from jax.experimental import pallas as pl
from jax.experimental.pallas import tpu as pltpu
from jax.sharding import Mesh
from jax.sharding import PartitionSpec as P

tanh_scale = math.sqrt(2.0 / math.pi)
cubic_term = 0.044715
eps_norm = 1e-06
bf16 = jnp.bfloat16
f32 = jnp.float32
PARTS = ((0, 1, 2, 3),)

COMP = ("zh", "core")
LON = ("x", "y")


def ring(count, step):
    return [(i, (i + step) % count) for i in range(count)]


def cross(step, x_core):
    pairs = []
    for c in range(2):
        for x in range(4):
            for y in range(4):
                to = (x, (y + step) % 4) if c != x_core else ((x + step) % 4, y)
                pairs.append((c * 16 + x * 4 + y, c * 16 + to[0] * 4 + to[1]))
    return pairs


def total_of(parts):
    own, one, two, three = [part.astype(f32) for part in parts]
    return (own + two) + (one + three)


def place(parts, index):
    return lax.dynamic_index_in_dim(parts, index, 0, keepdims=False)


def lat_halo(tile, lat):
    even = 1 - lax.rem(lat, 2)
    outer = lax.dynamic_slice_in_dim(tile, even, 3, 0)
    inner = lax.dynamic_slice_in_dim(tile, 1 - even, 3, 0)
    outer = lax.ppermute(outer, "lat", [(0, 1), (1, 0), (2, 3), (3, 2)])
    inner = lax.ppermute(inner, "lat", [(0, 0), (1, 2), (2, 1), (3, 3)])
    return outer, inner


def halo_rows(lat, outer_ref, inner_ref, fill):
    inside = jnp.where((lat == 1) | (lat == 2), 1.0, 0.0).astype(f32)

    @pl.when(lax.rem(lat, 2) == 1)
    def _():
        fill(0, outer_ref, None)
        fill(7, inner_ref, inside)

    @pl.when(lax.rem(lat, 2) == 0)
    def _():
        fill(0, inner_ref, inside)
        fill(7, outer_ref, None)


def picker(rows, cols, group, stride):
    row = lax.broadcasted_iota(jnp.int32, (rows, cols), 0)
    col = lax.broadcasted_iota(jnp.int32, (rows, cols), 1)
    pick = lax.rem(row, group) * stride + lax.div(row, group)
    return (pick == col).astype(f32).astype(bf16)


def mm(a, b, dims=((1,), (0,))):
    return lax.dot_general(a, b, (dims, ((), ())), preferred_element_type=f32)


def block_kernel(
    ocean_ref,
    outer_ref,
    own_ref,
    inner_ref,
    cot_ref,
    mask_ref,
    kern_ref,
    gain_ref,
    w_in_air,
    w_out_air,
    w_in_sea,
    w_out_sea,
    result_ref,
    to_0,
    to_1,
    to_2,
    to_3,
    gct_ref,
    w_in,
    w_out,
    taps_in,
    conv,
    normed,
    norm_in,
    norm_in_t,
    gb,
    branch,
    gnorm,
    small,
    packed,
    out_0,
    out_1,
    out_2,
    out_3,
    sems,
):
    outs = (out_0, out_1, out_2, out_3)
    targets = (to_0, to_1, to_2, to_3)

    def send(j, first, count, sem):
        rows = pl.ds(first, count)
        return pltpu.make_async_copy(outs[j].at[rows], targets[j].at[rows], sems.at[sem])

    here, far_step, near_step = ocean_ref[1], ocean_ref[2], ocean_ref[3]

    def weight_copies(expand, contract):
        copies = []
        for n in range(4):
            a, b = pl.ds(n * 128, 128), pl.ds(n * 512, 512)
            copies.append(pltpu.make_async_copy(expand.at[a], w_in.at[a], sems.at[n]))
            copies.append(pltpu.make_async_copy(contract.at[b], w_out.at[b], sems.at[n + 4]))
        return copies

    @pl.when(ocean_ref[0] == 1)
    def _():
        for copy in weight_copies(w_in_sea, w_out_sea):
            copy.start()

    @pl.when(ocean_ref[0] == 0)
    def _():
        for copy in weight_copies(w_in_air, w_out_air):
            copy.start()

    spread = picker(144, 96, 8, 12)

    def fill(first, source, factor, count=3):
        for r in range(count):
            q = mm(spread, source[r])
            q = q if factor is None else q * factor
            for lb in range(4):
                taps_in[lb, first + r] = q[:, lb * 128 : lb * 128 + 128].reshape(18, 8, 128)

    fill(3, own_ref, None, 4)
    halo_rows(ocean_ref[4], outer_ref, inner_ref, fill)
    order = picker(96, 96, 8, 12)
    for i in range(4):
        gb[i * 96 : i * 96 + 96, :] = mm(order, cot_ref[i]).astype(bf16)

    def conv_step(n, carry):
        lb, i = lax.div(n, 4), lax.rem(n, 4)
        acc = [None] * 12
        for u in range(7):
            q = [taps_in[lb, i + u, t] for t in range(18)]
            for v in range(7):
                k = kern_ref[lb, pl.ds(u * 7 + v, 1), :]
                for t in range(12):
                    term = k * q[t + v]
                    acc[t] = term if acc[t] is None else acc[t] + term
        lanes = pl.ds(pl.multiple_of(lb * 128, 128), 128)
        for t in range(12):
            conv[pl.ds(pl.multiple_of(i * 96 + t * 8, 8), 8), lanes] = acc[t]
        return carry

    lax.fori_loop(0, 16, conv_step, 0)

    gain = gain_ref[...]
    scales = []
    for i in range(4):
        rows = slice(i * 96, i * 96 + 96)
        c = conv[rows, :]
        centred = c - jnp.mean(c, axis=1, keepdims=True)
        scale = lax.rsqrt(jnp.mean(centred * centred, axis=1, keepdims=True) + eps_norm)
        z = centred * scale
        scales.append(scale)
        normed[rows, :] = z
        norm_in[rows, :] = (z * gain).astype(bf16)
    turned = norm_in[...].T
    for j in range(16):
        far = lax.rem(lax.div(j, far_step), 4)
        near = lax.rem(lax.div(j, near_step), 4)
        k = lax.rem(far + 4 - here, 4)
        rows = pl.ds(pl.multiple_of(k * 128 + near * 32, 32), 32)
        norm_in_t[rows, :] = turned[j * 32 : j * 32 + 32]
    branch[...] = jnp.zeros_like(branch)
    gnorm[...] = jnp.zeros_like(gnorm)
    for copy in weight_copies(w_in_air, w_out_air):
        copy.wait()

    for k in range(4):
        far = lax.rem(here + k, 4)
        blocks = [far * far_step + near * near_step for near in range(4)]
        picked = [pl.ds(pl.multiple_of(block * 128, 128), 128) for block in blocks]
        for p in PARTS:
            wi = jnp.concatenate([w_in[:, picked[q]] for q in p], axis=1)
            wo = jnp.concatenate([w_out[picked[q], :] for q in p], axis=0)
            pre = mm(norm_in[...], wi)
            square = pre * pre
            half = 0.5 + 0.5 * jnp.tanh(pre * (tanh_scale + (tanh_scale * cubic_term) * square))
            value = pre * half
            hidden = value.astype(bf16)
            slope = half + value * (1.0 - half) * (
                2.0 * tanh_scale + (6.0 * tanh_scale * cubic_term) * square
            )
            gpre = (mm(gb[...], wo, ((1,), (1,))) * slope).astype(bf16)
            branch[...] += mm(hidden, wo)
            gnorm[...] += mm(gpre, wi, ((1,), (1,)))
            gwi = mm(norm_in_t[...], gpre).astype(bf16)
            gwo = mm(hidden, gb[...], ((0,), (0,))).astype(bf16)
            for n, q in enumerate(p):
                lanes = pl.ds(pl.multiple_of(lax.rem(blocks[q], 4) * 128, 128), 128)
                band = lax.div(blocks[q], 4) * 32
                for j in range(4):
                    for near in range(4):
                        rows = pl.ds(pl.multiple_of(near * 256 + band, 32), 32)
                        outs[j][rows, lanes] = gwi[
                            j * 128 + near * 32 : j * 128 + near * 32 + 32,
                            n * 128 : n * 128 + 128,
                        ]
                outs[k][q * 256 + 128 : q * 256 + 256, :] = gwo[n * 128 : n * 128 + 128]
    for j in range(4):
        send(j, 0, 1024, 8 + j).start()

    back = picker(96, 96, 12, 8)
    ggain = jnp.zeros((1, 512), f32)
    for i in range(4):
        rows = slice(i * 96, i * 96 + 96)
        field = jnp.concatenate(
            [taps_in[lb, 3 + i, 3:15].reshape(96, 128) for lb in range(4)], axis=1
        )
        m = mask_ref[rows, :]
        res = (field + jnp.concatenate([m] * 4, axis=1) * branch[rows, :]).astype(bf16)
        result_ref[i] = mm(back, res).astype(bf16)[:90]
        g, z = gnorm[rows, :], normed[rows, :]
        ggain = ggain + jnp.sum(g * z, axis=0, keepdims=True)
        g = g * gain
        conv[rows, :] = scales[i] * (
            g - jnp.mean(g, axis=1, keepdims=True) - z * jnp.mean(g * z, axis=1, keepdims=True)
        )

    to_nat = picker(96, 96, 12, 8)
    to_16 = picker(96, 96, 16, 6)
    shuffle = mm(to_16, to_nat).astype(bf16)
    for i in range(4):
        rows = slice(i * 96, i * 96 + 96)
        moved = mm(shuffle, conv[rows, :].astype(bf16)).astype(bf16)
        norm_in[rows, :] = moved
    gct_ref[...] = norm_in[...].T

    def kern_step(n, carry):
        lb, u = lax.div(n, 7), lax.rem(n, 7)
        lanes = pl.ds(pl.multiple_of(lb * 128, 128), 128)
        acc = [jnp.zeros((8, 128), f32)] * 7
        for i in range(4):
            q = [taps_in[lb, i + u, t] for t in range(18)]
            for t in range(12):
                g = conv[i * 96 + t * 8 : i * 96 + t * 8 + 8, lanes]
                for v in range(7):
                    acc[v] = acc[v] + g * q[t + v]
        rows = [jnp.sum(a, axis=0, keepdims=True) for a in acc] + [jnp.zeros((1, 128), f32)]
        small[pl.ds(pl.multiple_of(u * 8, 8), 8), lanes] = jnp.concatenate(rows, axis=0)
        return carry

    lax.fori_loop(0, 28, kern_step, 0)
    for u in range(7):
        packed[u * 7 : u * 7 + 7, :] = small[u * 8 : u * 8 + 7, :]
    packed[49:50, :] = ggain
    packed[50:64, :] = jnp.zeros((14, 512), f32)
    for out in outs:
        out[1024:1088, :] = packed[...].astype(bf16)
    for j in range(4):
        send(j, 1024, 64, 12 + j).start()
    for j in range(4):
        send(j, 0, 1024, 8 + j).wait()
        send(j, 1024, 64, 12 + j).wait()


def block(ocean, outer, own, inner, cot, mask, kern, gain, wia, woa, wis, wos):
    vmem = pl.BlockSpec(memory_space=pltpu.VMEM)
    hbm = pl.BlockSpec(memory_space=pltpu.HBM)
    flops = 2 * 6 * 384 * 512 * 2048
    return pl.pallas_call(
        block_kernel,
        out_shape=(
            jax.ShapeDtypeStruct((4, 90, 512), bf16),
            *[jax.ShapeDtypeStruct((1088, 512), bf16)] * 4,
            jax.ShapeDtypeStruct((512, 384), bf16),
        ),
        in_specs=[pl.BlockSpec(memory_space=pltpu.SMEM)] + [vmem] * 7 + [hbm] * 4,
        out_specs=(vmem,) + (hbm,) * 4 + (vmem,),
        scratch_shapes=[
            pltpu.VMEM((512, 2048), bf16),
            pltpu.VMEM((2048, 512), bf16),
            pltpu.VMEM((4, 10, 18, 8, 128), f32),
            pltpu.VMEM((384, 512), f32),
            pltpu.VMEM((384, 512), f32),
            pltpu.VMEM((384, 512), bf16),
            pltpu.VMEM((512, 384), bf16),
            pltpu.VMEM((384, 512), bf16),
            pltpu.VMEM((384, 512), f32),
            pltpu.VMEM((384, 512), f32),
            pltpu.VMEM((56, 512), f32),
            pltpu.VMEM((64, 512), f32),
            *[pltpu.VMEM((1088, 512), bf16)] * 4,
            pltpu.SemaphoreType.DMA((16,)),
        ],
        compiler_params=pltpu.CompilerParams(vmem_limit_bytes=51 * 1024 * 1024),
        cost_estimate=pl.CostEstimate(
            flops=flops, bytes_accessed=12 * 1024 * 1024, transcendentals=384 * 2048
        ),
        name="block_kernel",
    )(ocean, outer, own, inner, cot, mask, kern, gain, wia, woa, wis, wos)


def couple_kernel(
    lat_ref,
    outer_ref,
    own_ref,
    inner_ref,
    gct_ref,
    cot_ref,
    kern_ref,
    scale_ref,
    out_ref,
    rows16,
    acc,
    gct,
    taps,
):
    spread = picker(192, 96, 16, 6)

    def fill(first, source, factor, count=3):
        for r in range(count):
            q = mm(spread, source[r])
            rows16[first + r] = (q if factor is None else q * factor).astype(bf16)

    fill(3, own_ref, None, 4)
    halo_rows(lat_ref[0], outer_ref, inner_ref, fill)
    order = picker(96, 96, 16, 6)
    moved = [mm(order, cot_ref[i]).astype(bf16) for i in range(4)]
    acc[...] = mm(jnp.concatenate(moved, axis=0).T, rows16[3:7, 48:144, :].reshape(384, 512))
    gct[...] = gct_ref[...].astype(f32)
    turned = kern_ref[...].T
    for u in range(7):
        taps[u] = turned[:, u * 8 : u * 8 + 8]

    def step(u, carry):
        left, right = [], []
        for v in range(7):
            left.append((taps[u, :, v : v + 1] * gct[...]).astype(bf16))
            right.append(rows16[pl.ds(u, 4), v * 16 : v * 16 + 96, :].reshape(384, 512))
        acc[...] += mm(jnp.concatenate(left, axis=1), jnp.concatenate(right, axis=0))
        return carry

    lax.fori_loop(0, 7, step, 0)
    out_ref[...] = (acc[...] * scale_ref[0]).astype(bf16).T


def couple(lat, outer, own, inner, gct, cot, kern, scale):
    vmem = pl.BlockSpec(memory_space=pltpu.VMEM)
    return pl.pallas_call(
        couple_kernel,
        out_shape=jax.ShapeDtypeStruct((512, 512), bf16),
        in_specs=[pl.BlockSpec(memory_space=pltpu.SMEM)]
        + [vmem] * 6
        + [pl.BlockSpec(memory_space=pltpu.SMEM)],
        out_specs=vmem,
        scratch_shapes=[
            pltpu.VMEM((10, 192, 512), bf16),
            pltpu.VMEM((512, 512), f32),
            pltpu.VMEM((512, 384), f32),
            pltpu.VMEM((7, 512, 8), f32),
        ],
        compiler_params=pltpu.CompilerParams(vmem_limit_bytes=24 * 1024 * 1024),
        cost_estimate=pl.CostEstimate(
            flops=2 * 50 * 384 * 512 * 512, bytes_accessed=4 * 1024 * 1024, transcendentals=0
        ),
        name="couple_kernel",
    )(lat, outer, own, inner, gct, cot, kern, scale)


def finish_kernel(place_ref, mine_ref, mine_beside_ref, across_ref, across_beside_ref, *refs):
    outs, total = refs[:10], refs[10]
    first_zh, first_core = place_ref[0] == 0, place_ref[1] == 0
    mine, across = mine_ref[...].astype(f32), across_ref[...].astype(f32)
    mine_beside = mine_beside_ref[...].astype(f32)
    across_beside = across_beside_ref[...].astype(f32)
    near = jnp.where(first_zh, mine, across)
    near_beside = jnp.where(first_zh, mine_beside, across_beside)
    far = jnp.where(first_zh, across, mine)
    far_beside = jnp.where(first_zh, across_beside, mine_beside)
    far_air = jnp.where(first_core, far, far_beside)
    total[0] = (near + near_beside) + far_air
    total[1] = jnp.where(first_core, far_beside, far)
    for n in range(2):
        kern_ref, gain_ref, expand_ref, contract_ref = outs[n * 4 : n * 4 + 4]
        kern_ref[...] = total[n, 64:113, :]
        gain_ref[...] = total[n, 113:114, :]
        for cb in range(4):
            expand_ref[:, cb * 512 : cb * 512 + 512] = total[n, cb * 8 : cb * 8 + 8, :]
        contract_ref[...] = total[n, 32:64, :]
        outs[8 + n][...] = total[n, 120:128, :]


def finish(here, mine, mine_beside, across, across_beside):
    vmem = pl.BlockSpec(memory_space=pltpu.VMEM)
    shapes = [(49, 512), (1, 512), (8, 2048), (32, 512)] * 2 + [(8, 512)] * 2
    return pl.pallas_call(
        finish_kernel,
        out_shape=[jax.ShapeDtypeStruct(shape, f32) for shape in shapes],
        in_specs=[pl.BlockSpec(memory_space=pltpu.SMEM)] + [vmem] * 4,
        out_specs=[vmem] * 10,
        scratch_shapes=[pltpu.VMEM((2, 128, 512), f32)],
        compiler_params=pltpu.CompilerParams(vmem_limit_bytes=8 * 1024 * 1024),
        name="finish_kernel",
    )(here, mine, mine_beside, across, across_beside)


def on_device(
    component_snapshots,
    cotangent,
    land,
    atmosphere_kernel,
    atmosphere_gain,
    atmosphere_expand_weight,
    atmosphere_contract_weight,
    ocean_kernel,
    ocean_gain,
    ocean_expand_weight,
    ocean_contract_weight,
    marine_to_air_map,
    flux_weight,
):
    zh, core = lax.axis_index("zh"), lax.axis_index("core")
    is_ocean = (zh == 1) & (core == 1)
    copies = 3.0
    sea = (1 - land).astype(f32)
    local = lax.optimization_barrier(component_snapshots)[0]

    def edge(columns):
        flags = jnp.broadcast_to(sea[:, columns].astype(bf16)[None, :, :, None], (1, 4, 3, 128))
        return jnp.concatenate([component_snapshots[:, :, columns], flags], axis=3)[0]

    west = lax.ppermute(edge(slice(87, 90)), LON, ring(16, 1))
    east = lax.ppermute(edge(slice(0, 3)), LON, ring(16, -1))
    local = jnp.concatenate([west[:, :, :512], local, east[:, :, :512]], axis=1)
    sea_wide = jnp.concatenate(
        [west[:, :, 512].astype(f32), sea, east[:, :, 512].astype(f32)], axis=1
    )

    beside = lax.ppermute(local, "core", ring(2, 1))
    pair_sum = (local.astype(f32) + beside.astype(f32)).astype(bf16)
    payload = jnp.where(zh == 0, pair_sum, jnp.where(core == 0, beside, local))
    half = lax.dynamic_slice_in_dim(payload, core * 2, 2, axis=0)
    got = lax.ppermute(half, "zh", ring(2, 1))
    coupling = jnp.where(is_ocean, flux_weight, marine_to_air_map)
    kernel = jnp.where(is_ocean, ocean_kernel, atmosphere_kernel)
    gain = jnp.where(is_ocean, ocean_gain, atmosphere_gain)
    mask = jnp.where(is_ocean, sea, jnp.ones_like(sea))
    grad_branch = (mask[:, :, None] * cotangent[0].astype(f32)).astype(bf16)
    grad_branch = jnp.pad(grad_branch, ((0, 0), (0, 6), (0, 0)))
    mask = jnp.pad(mask, ((0, 0), (0, 6))).reshape(4, 8, 12).transpose(0, 2, 1).reshape(384, 1)
    mask = jnp.broadcast_to(mask, (384, 128))
    kernel_lanes = kernel.reshape(49, 4, 128).transpose(1, 0, 2)
    kernel_rows = jnp.pad(kernel.reshape(7, 7, 512), ((0, 1), (0, 1), (0, 0))).reshape(64, 512)
    got, coupling, kernel_lanes, kernel_rows, gain, mask, grad_branch = lax.optimization_barrier(
        (got, coupling, kernel_lanes, kernel_rows, gain, mask, grad_branch)
    )
    got_beside = lax.ppermute(got, "core", ring(2, 1))
    full = jnp.where(
        core == 0,
        jnp.concatenate([got, got_beside], axis=0),
        jnp.concatenate([got_beside, got], axis=0),
    )
    ocean_sum = (full.astype(f32) + beside.astype(f32)).astype(bf16)
    partner = jnp.where(zh == 0, full, jnp.where(core == 0, beside, ocean_sum))

    projected = jnp.dot(partner.reshape(384, 512), coupling, preferred_element_type=f32)
    forcing = jnp.where(is_ocean, projected / copies, projected.astype(bf16).astype(f32))
    field = local.astype(f32) + sea_wide[:, :, None] * forcing.reshape(4, 96, 512)
    field = field.astype(bf16)
    lat = lax.axis_index("lat")
    outer, inner = lat_halo(field, lat)
    masked = (sea_wide[:, :, None] * partner.astype(f32)).astype(bf16)
    masked_outer, masked_inner = lat_halo(masked, lat)

    x, y = lax.axis_index("x"), lax.axis_index("y")
    result, *parts, grad_conv_t = block(
        jnp.stack(
            [
                is_ocean.astype(jnp.int32),
                jnp.where(core == 0, x, y),
                jnp.where(core == 0, 4, 1),
                jnp.where(core == 0, 1, 4),
                lat,
            ]
        ),
        outer,
        field,
        inner,
        grad_branch,
        mask,
        kernel_lanes,
        gain[None],
        atmosphere_expand_weight,
        atmosphere_contract_weight,
        ocean_expand_weight,
        ocean_contract_weight,
    )

    for k in (1, 2, 3):
        parts[k] = lax.ppermute(parts[k], ("core", "x", "y"), cross(k, 0))

    grad_couple = couple(
        lat.reshape(1),
        masked_outer,
        masked,
        masked_inner,
        grad_conv_t,
        grad_branch,
        kernel_rows,
        jnp.where(is_ocean, 1.0 / copies, 1.0).astype(f32).reshape(1),
    )
    small = total_of([part[1024:1080] for part in parts])
    near = jnp.where(core == 0, y, x)
    messages = []
    for k in range(4):
        start = lax.rem(near + k, 4) * 256
        table = total_of([lax.dynamic_slice_in_dim(part, start, 256, 0) for part in parts])
        messages.append(jnp.concatenate([table, small], axis=0).astype(bf16))
    for k in (1, 2, 3):
        messages[k] = lax.ppermute(messages[k], ("core", "x", "y"), cross(k, 1))
    shares = grad_couple.reshape(16, 4, 8, 512)
    shares = [
        lax.dynamic_index_in_dim(shares, lax.rem(lat + k, 4), 1, keepdims=False) for k in range(4)
    ]
    for k in (1, 2, 3):
        shares[k] = lax.ppermute(shares[k], "lat", ring(4, k))
    gathered = lax.all_to_all(total_of(shares).astype(bf16), LON, 0, 0, tiled=True)
    gathered = jnp.sum(gathered.astype(f32), axis=0)
    table = total_of(messages)

    pieces = jnp.concatenate(
        [
            table[:128].reshape(4, 4, 8, 512).transpose(1, 0, 2, 3).reshape(4, 32, 512),
            table[128:256].reshape(4, 32, 512),
            jnp.broadcast_to(table[256:][None], (4, 56, 512)),
        ],
        axis=1,
    ).astype(bf16)
    rows = [place(pieces, lax.rem(lat + k, 4)) for k in range(4)]
    for k in (1, 2, 3):
        rows[k] = lax.ppermute(rows[k], "lat", ring(4, k))
    mine = jnp.concatenate([total_of(rows), gathered], axis=0).astype(bf16)
    mine_beside = lax.ppermute(mine, "core", ring(2, 1))
    across = lax.ppermute(mine, "zh", ring(2, 1))
    across_beside = lax.ppermute(across, "core", ring(2, 1))
    outs = finish(jnp.stack([zh, core]), mine, mine_beside, across, across_beside)
    return (
        (result[None],)
        + (outs[0], outs[1].reshape(512), outs[2], outs[3])
        + (outs[4], outs[5].reshape(512), outs[6], outs[7])
        + (outs[8], outs[9])
    )


def solution(mesh):
    fine = Mesh(mesh.devices.reshape(2, 2, 4, 4, 4), ("zh", "core", "x", "y", "lat"))
    state = P(COMP, "lat", LON, None)
    rows = P(("x", "y", "lat"), None)
    in_specs = (state, state, P("lat", LON)) + (P(),) * 10
    out_specs = (state, P(), P(), rows, rows, P(), P(), rows, rows, rows, rows)
    return jax.shard_map(
        on_device, mesh=fine, in_specs=in_specs, out_specs=out_specs, check_vma=False
    )
```

```python
import math

import jax
import jax.numpy as jnp
from jax import lax
from jax.experimental import pallas as pl
from jax.experimental.pallas import tpu as pltpu
from jax.sharding import Mesh
from jax.sharding import PartitionSpec as P

tanh_scale = math.sqrt(2.0 / math.pi)
cubic_term = 0.044715
eps_norm = 1e-06
bf16 = jnp.bfloat16
f32 = jnp.float32
PARTS = ((0, 1, 2, 3),)

COMP = ("zh", "core")
LON = ("x", "y")


def ring(count, step):
    return [(i, (i + step) % count) for i in range(count)]


def cross(step, x_core):
    pairs = []
    for c in range(2):
        for x in range(4):
            for y in range(4):
                to = (x, (y + step) % 4) if c != x_core else ((x + step) % 4, y)
                pairs.append((c * 16 + x * 4 + y, c * 16 + to[0] * 4 + to[1]))
    return pairs


def total_of(parts):
    own, one, two, three = [part.astype(f32) for part in parts]
    return (own + two) + (one + three)


def place(parts, index):
    return lax.dynamic_index_in_dim(parts, index, 0, keepdims=False)


def lat_halo(tile, lat):
    even = 1 - lax.rem(lat, 2)
    outer = lax.dynamic_slice_in_dim(tile, even, 3, 0)
    inner = lax.dynamic_slice_in_dim(tile, 1 - even, 3, 0)
    outer = lax.ppermute(outer, "lat", [(0, 1), (1, 0), (2, 3), (3, 2)])
    inner = lax.ppermute(inner, "lat", [(0, 0), (1, 2), (2, 1), (3, 3)])
    return outer, inner


def halo_rows(lat, outer_ref, inner_ref, fill):
    inside = jnp.where((lat == 1) | (lat == 2), 1.0, 0.0).astype(f32)

    @pl.when(lax.rem(lat, 2) == 1)
    def _():
        fill(0, outer_ref, None)
        fill(7, inner_ref, inside)

    @pl.when(lax.rem(lat, 2) == 0)
    def _():
        fill(0, inner_ref, inside)
        fill(7, outer_ref, None)


def picker(rows, cols, group, stride):
    row = lax.broadcasted_iota(jnp.int32, (rows, cols), 0)
    col = lax.broadcasted_iota(jnp.int32, (rows, cols), 1)
    pick = lax.rem(row, group) * stride + lax.div(row, group)
    return (pick == col).astype(f32).astype(bf16)


def mm(a, b, dims=((1,), (0,))):
    return lax.dot_general(a, b, (dims, ((), ())), preferred_element_type=f32)


def block_kernel(
    ocean_ref,
    outer_ref,
    own_ref,
    inner_ref,
    cot_ref,
    mask_ref,
    kern_ref,
    gain_ref,
    w_in_air,
    w_out_air,
    w_in_sea,
    w_out_sea,
    result_ref,
    to_0,
    to_1,
    to_2,
    to_3,
    gct_ref,
    w_in,
    w_out,
    taps_in,
    conv,
    normed,
    norm_in,
    norm_in_t,
    gb,
    branch,
    gnorm,
    small,
    packed,
    out_0,
    out_1,
    out_2,
    out_3,
    sems,
):
    outs = (out_0, out_1, out_2, out_3)
    targets = (to_0, to_1, to_2, to_3)

    def send(j, first, count, sem):
        rows = pl.ds(first, count)
        return pltpu.make_async_copy(outs[j].at[rows], targets[j].at[rows], sems.at[sem])

    here, far_step, near_step = ocean_ref[1], ocean_ref[2], ocean_ref[3]

    def weight_copies(expand, contract):
        copies = []
        for n in range(4):
            a, b = pl.ds(n * 128, 128), pl.ds(n * 512, 512)
            copies.append(pltpu.make_async_copy(expand.at[a], w_in.at[a], sems.at[n]))
            copies.append(pltpu.make_async_copy(contract.at[b], w_out.at[b], sems.at[n + 4]))
        return copies

    @pl.when(ocean_ref[0] == 1)
    def _():
        for copy in weight_copies(w_in_sea, w_out_sea):
            copy.start()

    @pl.when(ocean_ref[0] == 0)
    def _():
        for copy in weight_copies(w_in_air, w_out_air):
            copy.start()

    spread = picker(144, 96, 8, 12)

    def fill(first, source, factor, count=3):
        for r in range(count):
            q = mm(spread, source[r])
            q = q if factor is None else q * factor
            for lb in range(4):
                taps_in[lb, first + r] = q[:, lb * 128 : lb * 128 + 128].reshape(18, 8, 128)

    fill(3, own_ref, None, 4)
    halo_rows(ocean_ref[4], outer_ref, inner_ref, fill)
    order = picker(96, 96, 8, 12)
    for i in range(4):
        gb[i * 96 : i * 96 + 96, :] = mm(order, cot_ref[i]).astype(bf16)

    def conv_step(n, carry):
        lb, i = lax.div(n, 4), lax.rem(n, 4)
        acc = [None] * 12
        for u in range(7):
            q = [taps_in[lb, i + u, t] for t in range(18)]
            for v in range(7):
                k = kern_ref[lb, pl.ds(u * 7 + v, 1), :]
                for t in range(12):
                    term = k * q[t + v]
                    acc[t] = term if acc[t] is None else acc[t] + term
        lanes = pl.ds(pl.multiple_of(lb * 128, 128), 128)
        for t in range(12):
            conv[pl.ds(pl.multiple_of(i * 96 + t * 8, 8), 8), lanes] = acc[t]
        return carry

    lax.fori_loop(0, 16, conv_step, 0)

    gain = gain_ref[...]
    scales = []
    for i in range(4):
        rows = slice(i * 96, i * 96 + 96)
        c = conv[rows, :]
        centred = c - jnp.mean(c, axis=1, keepdims=True)
        scale = lax.rsqrt(jnp.mean(centred * centred, axis=1, keepdims=True) + eps_norm)
        z = centred * scale
        scales.append(scale)
        normed[rows, :] = z
        norm_in[rows, :] = (z * gain).astype(bf16)
    turned = norm_in[...].T
    for j in range(16):
        far = lax.rem(lax.div(j, far_step), 4)
        near = lax.rem(lax.div(j, near_step), 4)
        k = lax.rem(far + 4 - here, 4)
        rows = pl.ds(pl.multiple_of(k * 128 + near * 32, 32), 32)
        norm_in_t[rows, :] = turned[j * 32 : j * 32 + 32]
    branch[...] = jnp.zeros_like(branch)
    gnorm[...] = jnp.zeros_like(gnorm)
    for copy in weight_copies(w_in_air, w_out_air):
        copy.wait()

    for k in range(4):
        far = lax.rem(here + k, 4)
        blocks = [far * far_step + near * near_step for near in range(4)]
        picked = [pl.ds(pl.multiple_of(block * 128, 128), 128) for block in blocks]
        for p in PARTS:
            wi = jnp.concatenate([w_in[:, picked[q]] for q in p], axis=1)
            wo = jnp.concatenate([w_out[picked[q], :] for q in p], axis=0)
            pre = mm(norm_in[...], wi)
            square = pre * pre
            half = 0.5 + 0.5 * jnp.tanh(pre * (tanh_scale + (tanh_scale * cubic_term) * square))
            value = pre * half
            hidden = value.astype(bf16)
            slope = half + value * (1.0 - half) * (
                2.0 * tanh_scale + (6.0 * tanh_scale * cubic_term) * square
            )
            gpre = (mm(gb[...], wo, ((1,), (1,))) * slope).astype(bf16)
            branch[...] += mm(hidden, wo)
            gnorm[...] += mm(gpre, wi, ((1,), (1,)))
            gwi = mm(norm_in_t[...], gpre).astype(bf16)
            gwo = mm(hidden, gb[...], ((0,), (0,))).astype(bf16)
            for n, q in enumerate(p):
                lanes = pl.ds(pl.multiple_of(lax.rem(blocks[q], 4) * 128, 128), 128)
                band = lax.div(blocks[q], 4) * 32
                for j in range(4):
                    for near in range(4):
                        rows = pl.ds(pl.multiple_of(near * 256 + band, 32), 32)
                        outs[j][rows, lanes] = gwi[
                            j * 128 + near * 32 : j * 128 + near * 32 + 32,
                            n * 128 : n * 128 + 128,
                        ]
                outs[k][q * 256 + 128 : q * 256 + 256, :] = gwo[n * 128 : n * 128 + 128]
    for j in range(4):
        send(j, 0, 1024, 8 + j).start()

    back = picker(96, 96, 12, 8)
    ggain = jnp.zeros((1, 512), f32)
    for i in range(4):
        rows = slice(i * 96, i * 96 + 96)
        field = jnp.concatenate(
            [taps_in[lb, 3 + i, 3:15].reshape(96, 128) for lb in range(4)], axis=1
        )
        m = mask_ref[rows, :]
        res = (field + jnp.concatenate([m] * 4, axis=1) * branch[rows, :]).astype(bf16)
        result_ref[i] = mm(back, res).astype(bf16)[:90]
        g, z = gnorm[rows, :], normed[rows, :]
        ggain = ggain + jnp.sum(g * z, axis=0, keepdims=True)
        g = g * gain
        conv[rows, :] = scales[i] * (
            g - jnp.mean(g, axis=1, keepdims=True) - z * jnp.mean(g * z, axis=1, keepdims=True)
        )

    to_nat = picker(96, 96, 12, 8)
    to_16 = picker(96, 96, 16, 6)
    shuffle = mm(to_16, to_nat).astype(bf16)
    for i in range(4):
        rows = slice(i * 96, i * 96 + 96)
        moved = mm(shuffle, conv[rows, :].astype(bf16)).astype(bf16)
        norm_in[rows, :] = moved
    gct_ref[...] = norm_in[...].T

    def kern_step(n, carry):
        lb, u = lax.div(n, 7), lax.rem(n, 7)
        lanes = pl.ds(pl.multiple_of(lb * 128, 128), 128)
        acc = [jnp.zeros((8, 128), f32)] * 7
        for i in range(4):
            q = [taps_in[lb, i + u, t] for t in range(18)]
            for t in range(12):
                g = conv[i * 96 + t * 8 : i * 96 + t * 8 + 8, lanes]
                for v in range(7):
                    acc[v] = acc[v] + g * q[t + v]
        rows = [jnp.sum(a, axis=0, keepdims=True) for a in acc] + [jnp.zeros((1, 128), f32)]
        small[pl.ds(pl.multiple_of(u * 8, 8), 8), lanes] = jnp.concatenate(rows, axis=0)
        return carry

    lax.fori_loop(0, 28, kern_step, 0)
    for u in range(7):
        packed[u * 7 : u * 7 + 7, :] = small[u * 8 : u * 8 + 7, :]
    packed[49:50, :] = ggain
    packed[50:64, :] = jnp.zeros((14, 512), f32)
    for out in outs:
        out[1024:1088, :] = packed[...].astype(bf16)
    for j in range(4):
        send(j, 1024, 64, 12 + j).start()
    for j in range(4):
        send(j, 0, 1024, 8 + j).wait()
        send(j, 1024, 64, 12 + j).wait()


def block(ocean, outer, own, inner, cot, mask, kern, gain, wia, woa, wis, wos):
    vmem = pl.BlockSpec(memory_space=pltpu.VMEM)
    hbm = pl.BlockSpec(memory_space=pltpu.HBM)
    flops = 2 * 6 * 384 * 512 * 2048
    return pl.pallas_call(
        block_kernel,
        out_shape=(
            jax.ShapeDtypeStruct((4, 90, 512), bf16),
            *[jax.ShapeDtypeStruct((1088, 512), bf16)] * 4,
            jax.ShapeDtypeStruct((512, 384), bf16),
        ),
        in_specs=[pl.BlockSpec(memory_space=pltpu.SMEM)] + [vmem] * 7 + [hbm] * 4,
        out_specs=(vmem,) + (hbm,) * 4 + (vmem,),
        scratch_shapes=[
            pltpu.VMEM((512, 2048), bf16),
            pltpu.VMEM((2048, 512), bf16),
            pltpu.VMEM((4, 10, 18, 8, 128), f32),
            pltpu.VMEM((384, 512), f32),
            pltpu.VMEM((384, 512), f32),
            pltpu.VMEM((384, 512), bf16),
            pltpu.VMEM((512, 384), bf16),
            pltpu.VMEM((384, 512), bf16),
            pltpu.VMEM((384, 512), f32),
            pltpu.VMEM((384, 512), f32),
            pltpu.VMEM((56, 512), f32),
            pltpu.VMEM((64, 512), f32),
            *[pltpu.VMEM((1088, 512), bf16)] * 4,
            pltpu.SemaphoreType.DMA((16,)),
        ],
        compiler_params=pltpu.CompilerParams(vmem_limit_bytes=51 * 1024 * 1024),
        cost_estimate=pl.CostEstimate(
            flops=flops, bytes_accessed=12 * 1024 * 1024, transcendentals=384 * 2048
        ),
        name="block_kernel",
    )(ocean, outer, own, inner, cot, mask, kern, gain, wia, woa, wis, wos)


def couple_kernel(
    lat_ref,
    outer_ref,
    own_ref,
    inner_ref,
    gct_ref,
    cot_ref,
    kern_ref,
    scale_ref,
    out_ref,
    rows16,
    acc,
    gct,
    taps,
):
    spread = picker(192, 96, 16, 6)

    def fill(first, source, factor, count=3):
        for r in range(count):
            q = mm(spread, source[r])
            rows16[first + r] = (q if factor is None else q * factor).astype(bf16)

    fill(3, own_ref, None, 4)
    halo_rows(lat_ref[0], outer_ref, inner_ref, fill)
    order = picker(96, 96, 16, 6)
    moved = [mm(order, cot_ref[i]).astype(bf16) for i in range(4)]
    acc[...] = mm(jnp.concatenate(moved, axis=0).T, rows16[3:7, 48:144, :].reshape(384, 512))
    gct[...] = gct_ref[...].astype(f32)
    turned = kern_ref[...].T
    for u in range(7):
        taps[u] = turned[:, u * 8 : u * 8 + 8]

    def step(u, carry):
        left, right = [], []
        for v in range(7):
            left.append((taps[u, :, v : v + 1] * gct[...]).astype(bf16))
            right.append(rows16[pl.ds(u, 4), v * 16 : v * 16 + 96, :].reshape(384, 512))
        acc[...] += mm(jnp.concatenate(left, axis=1), jnp.concatenate(right, axis=0))
        return carry

    lax.fori_loop(0, 7, step, 0)
    out_ref[...] = (acc[...] * scale_ref[0]).astype(bf16).T


def couple(lat, outer, own, inner, gct, cot, kern, scale):
    vmem = pl.BlockSpec(memory_space=pltpu.VMEM)
    return pl.pallas_call(
        couple_kernel,
        out_shape=jax.ShapeDtypeStruct((512, 512), bf16),
        in_specs=[pl.BlockSpec(memory_space=pltpu.SMEM)]
        + [vmem] * 6
        + [pl.BlockSpec(memory_space=pltpu.SMEM)],
        out_specs=vmem,
        scratch_shapes=[
            pltpu.VMEM((10, 192, 512), bf16),
            pltpu.VMEM((512, 512), f32),
            pltpu.VMEM((512, 384), f32),
            pltpu.VMEM((7, 512, 8), f32),
        ],
        compiler_params=pltpu.CompilerParams(vmem_limit_bytes=24 * 1024 * 1024),
        cost_estimate=pl.CostEstimate(
            flops=2 * 50 * 384 * 512 * 512, bytes_accessed=4 * 1024 * 1024, transcendentals=0
        ),
        name="couple_kernel",
    )(lat, outer, own, inner, gct, cot, kern, scale)


def finish_kernel(place_ref, mine_ref, mine_beside_ref, across_ref, across_beside_ref, *refs):
    outs, total = refs[:10], refs[10]
    first_zh, first_core = place_ref[0] == 0, place_ref[1] == 0
    mine, across = mine_ref[...].astype(f32), across_ref[...].astype(f32)
    mine_beside = mine_beside_ref[...].astype(f32)
    across_beside = across_beside_ref[...].astype(f32)
    near = jnp.where(first_zh, mine, across)
    near_beside = jnp.where(first_zh, mine_beside, across_beside)
    far = jnp.where(first_zh, across, mine)
    far_beside = jnp.where(first_zh, across_beside, mine_beside)
    far_air = jnp.where(first_core, far, far_beside)
    total[0] = (near + near_beside) + far_air
    total[1] = jnp.where(first_core, far_beside, far)
    for n in range(2):
        kern_ref, gain_ref, expand_ref, contract_ref = outs[n * 4 : n * 4 + 4]
        kern_ref[...] = total[n, 64:113, :]
        gain_ref[...] = total[n, 113:114, :]
        for cb in range(4):
            expand_ref[:, cb * 512 : cb * 512 + 512] = total[n, cb * 8 : cb * 8 + 8, :]
        contract_ref[...] = total[n, 32:64, :]
        outs[8 + n][...] = total[n, 114:122, :]


def finish(here, mine, mine_beside, across, across_beside):
    vmem = pl.BlockSpec(memory_space=pltpu.VMEM)
    shapes = [(49, 512), (1, 512), (8, 2048), (32, 512)] * 2 + [(8, 512)] * 2
    return pl.pallas_call(
        finish_kernel,
        out_shape=[jax.ShapeDtypeStruct(shape, f32) for shape in shapes],
        in_specs=[pl.BlockSpec(memory_space=pltpu.SMEM)] + [vmem] * 4,
        out_specs=[vmem] * 10,
        scratch_shapes=[pltpu.VMEM((2, 122, 512), f32)],
        compiler_params=pltpu.CompilerParams(vmem_limit_bytes=8 * 1024 * 1024),
        name="finish_kernel",
    )(here, mine, mine_beside, across, across_beside)


def on_device(
    component_snapshots,
    cotangent,
    land,
    atmosphere_kernel,
    atmosphere_gain,
    atmosphere_expand_weight,
    atmosphere_contract_weight,
    ocean_kernel,
    ocean_gain,
    ocean_expand_weight,
    ocean_contract_weight,
    marine_to_air_map,
    flux_weight,
):
    zh, core = lax.axis_index("zh"), lax.axis_index("core")
    is_ocean = (zh == 1) & (core == 1)
    copies = 3.0
    sea = (1 - land).astype(f32)
    local = lax.optimization_barrier(component_snapshots)[0]

    def edge(columns):
        flags = jnp.broadcast_to(sea[:, columns].astype(bf16)[None, :, :, None], (1, 4, 3, 128))
        return jnp.concatenate([component_snapshots[:, :, columns], flags], axis=3)[0]

    west = lax.ppermute(edge(slice(87, 90)), LON, ring(16, 1))
    east = lax.ppermute(edge(slice(0, 3)), LON, ring(16, -1))
    local = jnp.concatenate([west[:, :, :512], local, east[:, :, :512]], axis=1)
    sea_wide = jnp.concatenate(
        [west[:, :, 512].astype(f32), sea, east[:, :, 512].astype(f32)], axis=1
    )

    beside = lax.ppermute(local, "core", ring(2, 1))
    pair_sum = (local.astype(f32) + beside.astype(f32)).astype(bf16)
    payload = jnp.where(zh == 0, pair_sum, jnp.where(core == 0, beside, local))
    half = lax.dynamic_slice_in_dim(payload, core * 2, 2, axis=0)
    got = lax.ppermute(half, "zh", ring(2, 1))
    coupling = jnp.where(is_ocean, flux_weight, marine_to_air_map)
    kernel = jnp.where(is_ocean, ocean_kernel, atmosphere_kernel)
    gain = jnp.where(is_ocean, ocean_gain, atmosphere_gain)
    mask = jnp.where(is_ocean, sea, jnp.ones_like(sea))
    grad_branch = (mask[:, :, None] * cotangent[0].astype(f32)).astype(bf16)
    grad_branch = jnp.pad(grad_branch, ((0, 0), (0, 6), (0, 0)))
    mask = jnp.pad(mask, ((0, 0), (0, 6))).reshape(4, 8, 12).transpose(0, 2, 1).reshape(384, 1)
    mask = jnp.broadcast_to(mask, (384, 128))
    kernel_lanes = kernel.reshape(49, 4, 128).transpose(1, 0, 2)
    kernel_rows = jnp.pad(kernel.reshape(7, 7, 512), ((0, 1), (0, 1), (0, 0))).reshape(64, 512)
    got, coupling, kernel_lanes, kernel_rows, gain, mask, grad_branch = lax.optimization_barrier(
        (got, coupling, kernel_lanes, kernel_rows, gain, mask, grad_branch)
    )
    got_beside = lax.ppermute(got, "core", ring(2, 1))
    full = jnp.where(
        core == 0,
        jnp.concatenate([got, got_beside], axis=0),
        jnp.concatenate([got_beside, got], axis=0),
    )
    ocean_sum = (full.astype(f32) + beside.astype(f32)).astype(bf16)
    partner = jnp.where(zh == 0, full, jnp.where(core == 0, beside, ocean_sum))

    projected = jnp.dot(partner.reshape(384, 512), coupling, preferred_element_type=f32)
    forcing = jnp.where(is_ocean, projected / copies, projected.astype(bf16).astype(f32))
    field = local.astype(f32) + sea_wide[:, :, None] * forcing.reshape(4, 96, 512)
    field = field.astype(bf16)
    lat = lax.axis_index("lat")
    outer, inner = lat_halo(field, lat)
    masked = (sea_wide[:, :, None] * partner.astype(f32)).astype(bf16)
    masked_outer, masked_inner = lat_halo(masked, lat)

    x, y = lax.axis_index("x"), lax.axis_index("y")
    result, *parts, grad_conv_t = block(
        jnp.stack(
            [
                is_ocean.astype(jnp.int32),
                jnp.where(core == 0, x, y),
                jnp.where(core == 0, 4, 1),
                jnp.where(core == 0, 1, 4),
                lat,
            ]
        ),
        outer,
        field,
        inner,
        grad_branch,
        mask,
        kernel_lanes,
        gain[None],
        atmosphere_expand_weight,
        atmosphere_contract_weight,
        ocean_expand_weight,
        ocean_contract_weight,
    )

    for k in (1, 2, 3):
        parts[k] = lax.ppermute(parts[k], ("core", "x", "y"), cross(k, 0))

    grad_couple = couple(
        lat.reshape(1),
        masked_outer,
        masked,
        masked_inner,
        grad_conv_t,
        grad_branch,
        kernel_rows,
        jnp.where(is_ocean, 1.0 / copies, 1.0).astype(f32).reshape(1),
    )
    small = total_of([part[1024:1074] for part in parts])
    near = jnp.where(core == 0, y, x)
    messages = []
    for k in range(4):
        start = lax.rem(near + k, 4) * 256
        table = total_of([lax.dynamic_slice_in_dim(part, start, 256, 0) for part in parts])
        messages.append(jnp.concatenate([table, small], axis=0).astype(bf16))
    for k in (1, 2, 3):
        messages[k] = lax.ppermute(messages[k], ("core", "x", "y"), cross(k, 1))
    shares = grad_couple.reshape(16, 4, 8, 512)
    shares = [
        lax.dynamic_index_in_dim(shares, lax.rem(lat + k, 4), 1, keepdims=False) for k in range(4)
    ]
    for k in (1, 2, 3):
        shares[k] = lax.ppermute(shares[k], "lat", ring(4, k))
    gathered = lax.all_to_all(total_of(shares).astype(bf16), LON, 0, 0, tiled=True)
    gathered = jnp.sum(gathered.astype(f32), axis=0)
    table = total_of(messages)

    pieces = jnp.concatenate(
        [
            table[:128].reshape(4, 4, 8, 512).transpose(1, 0, 2, 3).reshape(4, 32, 512),
            table[128:256].reshape(4, 32, 512),
            jnp.broadcast_to(table[256:][None], (4, 50, 512)),
        ],
        axis=1,
    ).astype(bf16)
    rows = [place(pieces, lax.rem(lat + k, 4)) for k in range(4)]
    for k in (1, 2, 3):
        rows[k] = lax.ppermute(rows[k], "lat", ring(4, k))
    mine = jnp.concatenate([total_of(rows), gathered], axis=0).astype(bf16)
    mine_beside = lax.ppermute(mine, "core", ring(2, 1))
    across = lax.ppermute(mine, "zh", ring(2, 1))
    across_beside = lax.ppermute(across, "core", ring(2, 1))
    outs = finish(jnp.stack([zh, core]), mine, mine_beside, across, across_beside)
    return (
        (result[None],)
        + (outs[0], outs[1].reshape(512), outs[2], outs[3])
        + (outs[4], outs[5].reshape(512), outs[6], outs[7])
        + (outs[8], outs[9])
    )


def solution(mesh):
    fine = Mesh(mesh.devices.reshape(2, 2, 4, 4, 4), ("zh", "core", "x", "y", "lat"))
    state = P(COMP, "lat", LON, None)
    rows = P(("x", "y", "lat"), None)
    in_specs = (state, state, P("lat", LON)) + (P(),) * 10
    out_specs = (state, P(), P(), rows, rows, P(), P(), rows, rows, rows, rows)
    return jax.shard_map(
        on_device, mesh=fine, in_specs=in_specs, out_specs=out_specs, check_vma=False
    )
```
